256 devices in a mesh: dp: 32 (over y, x, core), tensor: 8 (over z).
Axes of the slice: x: 4, y: 4, z: 8, core: 2. Of those that a mesh axis runs over, the one named last changes fastest.
Arguments:
- heads_out: bfloat16 [32768, 3072], P('dp', 'tensor'), may hold values from -120 to 120, as said below
- grad_out: bfloat16 [32768, 6144], P(('dp', 'tensor')), may hold values from -0.1875 to 0.1875
- error: bfloat16 [32, 3072, 6144], P('dp', 'tensor'), may hold values from -6 to 6
- q_warm: float32 [8, 64, 6144], P('tensor'), may hold values from -6 to 6
Outputs:
- p_factor: float32 [64, 3072], P(None, 'tensor')
- q_factor: float32 [8, 64, 6144], P('tensor', None, 'dp')
- error_new: bfloat16 [32, 3072, 6144], P('dp', 'tensor')
The draws below stay inside these ranges and needn't reach their ends.
Inputs may be any that keep to these rules, and one draw needn't show every extreme that they name: `heads_out`: attention outputs of bounded magnitude.
All inputs are finite; a program needn't handle non-finite values.
Results may differ from the reference program's by a relative error of at most 0.0045.
Values may be sent and summed in bfloat16 or wider, within the bound.
A program may use at most 128 MiB of HBM per device.

```python
import jax
import jax.numpy as jnp
from jax import lax

D = 6144
H = 24
HD = 128
R = 64
TOK_DEV = 1024
TOKENS = 32768
N_DP = 32
N_TENSOR = 8


def draw_heads_out(key, part):
    key = jax.random.fold_in(key, 11)
    key_col = jax.random.fold_in(key, 0)
    key_base = jax.random.fold_in(key, 2)
    columns = H * HD
    place = jnp.arange(columns, dtype=jnp.float32) / (columns - 1)
    rising = 3.0 ** (0.5 * place)
    spread = jnp.exp(jax.random.uniform(key_col, (columns,), jnp.float32) * jnp.log(10.0))
    base = jnp.clip(jax.random.normal(key_base, (TOKENS, columns), jnp.float32), -4.0, 4.0)
    return (base * (rising * spread)[None, :] / 3.0).astype(jnp.bfloat16)


def levels(stream_key, dims, cuts, low, high):
    def one(axis_at, parts):
        draws = jax.random.uniform(jax.random.fold_in(jax.random.fold_in(stream_key, 6), axis_at), (parts,), jnp.float32, low / len(cuts), high / len(cuts))
        return jnp.repeat(jnp.exp(draws), dims[axis_at] // parts).reshape((-1,) + (1,) * (len(dims) - axis_at - 1))

    level = one(*cuts[0])
    for cut in cuts[1:]:
        level = level * one(*cut)
    return level


def bell_draw(rng, dims, scale, most, cuts=(), kind=jnp.bfloat16):
    result = jax.random.normal(rng, dims, jnp.float32) * scale
    if len(cuts) > 0:
        result = levels(rng, dims, cuts, -0.22, 0.18) * result
    return jnp.clip(result, min=-most, max=most).astype(kind)


def setup_inputs(seed: int = 0) -> dict:
    arg_keys = jax.random.split(jax.random.key(seed), 5)
    heads_out = draw_heads_out(jax.random.fold_in(arg_keys[4], 71), 0)
    grad_out = bell_draw(arg_keys[1], (TOKENS, D), (TOK_DEV ** -0.5), 0.1875, ((0, 256),))
    error = bell_draw(arg_keys[2], (N_DP, H * HD, D), 1.0, 6.0, ((0, 32), (1, 8)))
    q_warm = bell_draw(arg_keys[3], (N_TENSOR, R, D), 1.0, 6.0, ((0, 8),), jnp.float32)
    return {"heads_out": heads_out, "grad_out": grad_out, "error": error, "q_warm": q_warm}


def reference(heads_out, grad_out, error, q_warm):
    rows_group = H * HD // N_TENSOR

    def merged_block(index):
        start = index * TOK_DEV
        tokens = lax.dynamic_slice_in_dim(heads_out, start, TOK_DEV, 0)
        grads = lax.dynamic_slice_in_dim(grad_out, start, TOK_DEV, 0)
        product = jnp.dot(tokens.T.astype(jnp.float32), grads.astype(jnp.float32), preferred_element_type=jnp.float32)
        return product + error[index].astype(jnp.float32)
    merged = lax.map(merged_block, jnp.arange(N_DP, dtype=jnp.int32))
    shards = merged.reshape(N_DP, N_TENSOR, rows_group, D)
    total_p = jnp.einsum('ktid,trd->tir', shards, q_warm, precision=lax.Precision.HIGHEST)
    gram = jnp.einsum('tir,tis->trs', total_p, total_p, precision=lax.Precision.HIGHEST)
    lower = jnp.linalg.cholesky(gram)
    basis = jax.vmap(lambda fac, rhs: jax.scipy.linalg.solve_triangular(fac, rhs, lower=True))(lower, jnp.swapaxes(total_p, 1, 2))
    factor = jnp.einsum('tri,ktid->trd', basis, shards, precision=lax.Precision.HIGHEST) / N_DP
    energy = jnp.sum(factor * factor)
    scale = lax.rsqrt(energy / (H * HD * D) + 1e-06)
    approx = jnp.einsum('tri,trd->tid', basis, factor, precision=lax.Precision.HIGHEST).reshape(H * HD, D)
    error_new = (merged - approx[None]).astype(jnp.bfloat16)
    p_factor = jnp.swapaxes(basis, 0, 1).reshape(R, H * HD)
    return (p_factor, factor * scale, error_new)
```

```python
import functools

import jax
import jax.numpy as jnp
from jax import lax
from jax.experimental import pallas as pl
from jax.experimental.pallas import tpu as pltpu
from jax.sharding import PartitionSpec as P

MESH = pl.DeviceIdType.MESH
F32 = jnp.float32
BF16 = jnp.bfloat16


def split(value):
    high = value.astype(BF16)
    return high, (value - high.astype(F32)).astype(BF16)


def dot(a, b, a_dim, b_dim, **options):
    return lax.dot_general(a, b, (((a_dim,), (b_dim,)), ((), ())), preferred_element_type=F32, **options)


def orthonormal(ch, rows, cols):
    lanes = lax.broadcasted_iota(jnp.int32, (rows, 128), 1)
    del lanes

    def block(r, carry):
        start = pl.multiple_of(r * 8, 8)
        top = ch[pl.ds(start, 8), :]
        near = pltpu.roll(top[:, cols:], (128 - r * 8) % 128, 1)
        place = lax.broadcasted_iota(jnp.int32, (8, 1), 0)
        for i in range(8):
            inverse = lax.rsqrt(near[i : i + 1, i : i + 1])
            row, row_near = top[i : i + 1, :] * inverse, near[i : i + 1, :] * inverse
            column = jnp.where(place > i, near[:, i : i + 1] * inverse, 0.0)
            top = jnp.where(place == i, row, top - column * row)
            near = jnp.where(place == i, row_near, near - column * row_near)
        ch[pl.ds(start, 8), :] = top
        change = dot(top[:, cols : cols + rows], top, 0, 0, precision=lax.Precision.HIGHEST)
        below = lax.broadcasted_iota(jnp.int32, (rows, 1), 0) >= (r + 1) * 8
        ch[...] = jnp.where(below, ch[...] - change, ch[...])
        return carry

    lax.fori_loop(0, rows // 8, block, 0)


def kernel(
    sizes, heads, grad, err, q, p_out, q_out, e_out,
    own, gath, hv, at, ev, acc, qv, qs, g, pe, pt, pc, px, py, pf, ch,
    f, fc, xa, sa, ya, yb, sb, xb, ff, en,
    in_sem, out_sem, ring_send, ring_recv, p_send, p_recv, f_send, f_recv, c_send, c_recv, e_send, e_recv,
):
    ny, nx, nz = sizes
    nc = 2 * ny
    bk, w = own.shape[1], own.shape[2]
    rank = qv.shape[1]
    half = rank // 2
    eighth = half // nx
    hop = nz // 2
    replicas = ny * nx * 2
    k, z = lax.axis_index("dp"), lax.axis_index("tensor")
    core, x, y = k % 2, (k // 2) % nx, k // (2 * nx)

    def at_dp(y_to, x_to, core_to):
        return ((y_to * nx + x_to) * 2 + core_to, z)

    other_core = at_dp(y, x, 1 - core)
    x_peer = [None] + [at_dp(y, (x + d) % nx, core) for d in range(1, nx)]
    y_peer = [None] + [at_dp((y + d) % ny, x, core) for d in range(1, ny)]
    z_peer = [None] + [(k, (z + d) % nz) for d in range(1, nz)]

    def remote(src, dst, send, recv, device):
        return pltpu.make_async_remote_copy(
            src_ref=src, dst_ref=dst, send_sem=send, recv_sem=recv, device_id=device, device_id_type=MESH
        )

    def chunk_loop(body, count=nc):
        def step(c, carry):
            body(c)
            return carry

        lax.fori_loop(0, count, step, 0)

    def cols(c):
        return pl.ds(pl.multiple_of(c * w, w), w)

    def load_own(c):
        return pltpu.make_async_copy(grad.at[:, cols(c)], own.at[c], in_sem.at[0, c])

    def load_err(c):
        return pltpu.make_async_copy(err.at[0, :, cols(c)], ev.at[c], in_sem.at[1, c])

    def load_q(c):
        return pltpu.make_async_copy(q.at[0, :, cols(c)], qv.at[c], in_sem.at[2, c])

    load_heads = pltpu.make_async_copy(heads, hv, in_sem.at[3, 0])

    barrier = pltpu.get_barrier_semaphore()
    everyone = [other_core] + x_peer[1:] + y_peer[1:] + z_peer[1:]
    for device in everyone:
        pl.semaphore_signal(barrier, inc=1, device_id=device, device_id_type=MESH)

    load_heads.start()

    @chunk_loop
    def _(c):
        load_own(c).start()
        load_q(c).start()
        load_err(c).start()

    pl.semaphore_wait(barrier, len(everyone))

    far = 2 * (hop - 1)

    def slot(way, s):
        return way * (hop - 1) + s - 1

    def ring(way, s, c):
        part = pl.ds(way * (bk // 2), bk // 2)
        if s == 0:
            src = grad.at[:, cols(c)]
        else:
            src = gath.at[slot(way, s), c]
        if s == hop - 1:
            if s == 0:
                src = grad.at[part, cols(c)]
            else:
                src = gath.at[slot(way, s), c, part]
            dst = gath.at[far, c, part]
        else:
            dst = gath.at[slot(way, s + 1), c]
        return remote(src, dst, ring_send.at[way, s, c], ring_recv.at[way, s, c], z_peer[1] if way == 0 else z_peer[nz - 1])

    @chunk_loop
    def _(c):
        ring(0, 0, c).start()
        ring(1, 0, c).start()

    load_heads.wait()

    def flip(i, carry):
        at[i] = hv[pl.ds(pl.multiple_of(i * bk, bk), bk), :].astype(F32).T.astype(BF16)
        return carry

    lax.fori_loop(0, nz, flip, 0)
    g[...] = jnp.zeros_like(g)
    pe[...] = jnp.zeros_like(pe)

    def use(block, c, which):
        acc[c] += dot(at[which], block, 1, 0)
        place = pl.ds(pl.multiple_of(which * bk, bk), bk)
        g[:, place] += dot(qs[c], block, 1, 1)

    @chunk_loop
    def _(c):
        load_q(c).wait()
        high, low = split(qv[c])
        qs[c, 0:rank, :] = high
        qs[c, rank:, :] = low
        load_err(c).wait()
        acc[c] = ev[c].astype(F32)
        pe[...] += dot(qs[c], ev[c], 1, 1)
        load_own(c).wait()
        use(own[c], c, z)

    for s in range(1, hop):
        @chunk_loop
        def _(c):
            ring(0, s - 1, c).wait_recv()
            ring(0, s, c).start()
            ring(1, s - 1, c).wait_recv()
            ring(1, s, c).start()
            use(gath[slot(0, s), c], c, (z - s + nz) % nz)
            use(gath[slot(1, s), c], c, (z + s) % nz)

    @chunk_loop
    def _(c):
        ring(0, hop - 1, c).wait_recv()
        ring(1, hop - 1, c).wait_recv()
        use(gath[far, c], c, (z + hop) % nz)

    total = g[0:rank, :] + g[rank:, :]
    high, low = split(total)
    terms = dot(jnp.concatenate([high, low], axis=0), hv[...], 1, 0) + pe[...]
    pt[...] = terms[0:rank, :] + terms[rank:, :]
    mine = pl.ds(pl.multiple_of(core * half, half), half)
    theirs = pl.ds(pl.multiple_of((1 - core) * half, half), half)
    copy = remote(pt.at[theirs], pc, p_send.at[0], p_recv.at[0], other_core)
    copy.start()
    copy.wait()
    px[x] = pt[mine, :] + pc[...]
    copies = [remote(px.at[x], px.at[x], p_send.at[d], p_recv.at[d], x_peer[d]) for d in range(1, nx)]
    for copy in copies:
        copy.start()
    for copy in copies:
        copy.wait()
    py[y] = functools.reduce(lambda a, b: a + b, [px[i] for i in range(nx)])
    copies = [remote(py.at[y], py.at[y], p_send.at[nx + d], p_recv.at[nx + d], y_peer[d]) for d in range(1, ny)]
    for copy in copies:
        copy.start()
    for copy in copies:
        copy.wait()
    pf[mine, :] = functools.reduce(lambda a, b: a + b, [py[i] for i in range(ny)])
    copy = remote(pf.at[mine], pf.at[mine], p_send.at[nx], p_recv.at[nx], other_core)
    copy.start()
    copy.wait()

    m = pf.shape[1]
    ch[:, 0:m] = pf[...]
    ch[:, m:] = jnp.zeros((rank, 128), F32)
    ch[:, m : m + rank] = dot(pf[...], pf[...], 1, 1, precision=lax.Precision.HIGHEST)
    orthonormal(ch, rank, m)
    basis = ch[:, 0:m]
    p_out[...] = basis
    b_high, b_low = split(basis)
    b_both = jnp.concatenate([b_high, b_low], axis=0)

    def core_copy(c):
        return remote(f.at[c, theirs], fc.at[c], c_send.at[c], c_recv.at[c], other_core)

    @chunk_loop
    def _(c):
        high, low = split(acc[c])
        both = dot(b_both, high, 1, 0)
        f[c] = (both[0:rank] + both[rank:] + dot(b_high, low, 1, 0)) * (1.0 / replicas)
        core_copy(c).start()

    @chunk_loop
    def _(c):
        core_copy(c).wait()
        f[c, mine, :] += fc[c]

    def rows_of(x_at):
        return pl.ds(pl.multiple_of(core * half + x_at * eighth, eighth), eighth)

    rows = rows_of(x)
    first = pl.ds(0, ny)
    copies = [
        remote(f.at[first, rows_of((x + d) % nx)], xa.at[x], f_send.at[0, d], f_recv.at[0, d], x_peer[d])
        for d in range(1, nx)
    ] + [
        remote(f.at[ny + (y + d) % ny, mine], yb.at[y], f_send.at[1, d], f_recv.at[1, d], y_peer[d])
        for d in range(1, ny)
    ]
    for copy in copies:
        copy.start()
    xa[x] = f[first, rows, :]
    yb[y] = f[ny + y, mine, :]
    for copy in copies:
        copy.wait()
    sa[...] = functools.reduce(lambda a, b: a + b, [xa[i] for i in range(nx)])
    sb[...] = functools.reduce(lambda a, b: a + b, [yb[i] for i in range(ny)])

    copies = [
        remote(sa.at[(y + d) % ny], ya.at[y], f_send.at[2, d], f_recv.at[2, d], y_peer[d]) for d in range(1, ny)
    ] + [
        remote(sb.at[pl.ds(pl.multiple_of(((x + d) % nx) * eighth, eighth), eighth)], xb.at[x], f_send.at[3, d], f_recv.at[3, d], x_peer[d])
        for d in range(1, nx)
    ]
    for copy in copies:
        copy.start()
    ya[y] = sa[y]
    xb[x] = sb[pl.ds(pl.multiple_of(x * eighth, eighth), eighth), :]
    for copy in copies:
        copy.wait()
    ff[y, rows, :] = functools.reduce(lambda a, b: a + b, [ya[i] for i in range(ny)])
    ff[ny + y, rows, :] = functools.reduce(lambda a, b: a + b, [xb[i] for i in range(nx)])

    def spread(place, number, peers):
        return [remote(ff.at[place], ff.at[place], f_send.at[number, d], f_recv.at[number, d], peers[d]) for d in range(1, len(peers))]

    for pair in (
        spread((y, rows), 4, y_peer) + spread((ny + y, rows), 5, x_peer),
        spread((first, rows), 6, x_peer) + spread((ny + y, mine), 7, y_peer),
    ):
        for copy in pair:
            copy.start()
        for copy in pair:
            copy.wait()
    everything = pl.ds(0, nc)
    copy = remote(ff.at[everything, mine], ff.at[everything, mine], p_send.at[nx + ny], p_recv.at[nx + ny], other_core)
    copy.start()
    copy.wait()

    def squares(c, carry):
        return carry + jnp.sum(ff[c] * ff[c], axis=(0, 1), keepdims=True)

    energy = lax.fori_loop(0, nc, squares, jnp.zeros((1, 1), F32))
    en[z] = jnp.broadcast_to(energy, (8, 128))
    energies = [remote(en.at[z], en.at[z], e_send.at[d], e_recv.at[d], z_peer[d]) for d in range(1, nz)]
    for copy in energies:
        copy.start()

    b_wide = jnp.concatenate([b_high, b_high, b_low], axis=0).astype(F32).T.astype(BF16)

    def store(c):
        return pltpu.make_async_copy(ev.at[c], e_out.at[0, :, cols(c)], out_sem.at[c])

    @chunk_loop
    def _(c):
        high, low = split(ff[c])
        approx = dot(b_wide, jnp.concatenate([high, low, high], axis=0), 1, 0)
        ev[c] = (acc[c] - approx).astype(BF16)
        store(c).start()

    for copy in energies:
        copy.wait()
    entire = functools.reduce(lambda a, b: a + b, [en[i] for i in range(nz)])[0:1, 0:1]
    scale = lax.rsqrt(entire * (1.0 / (m * nz * w * nc)) + 1e-06)
    width = q_out.shape[2]
    piece = ff[k // nx]
    piece = pltpu.roll(piece, (w - (k % nx) * width) % w, 1)
    q_out[0] = piece[:, 0:width] * scale

    for s in range(hop):
        @chunk_loop
        def _(c):
            ring(0, s, c).wait_send()
            ring(1, s, c).wait_send()

    @chunk_loop
    def _(c):
        store(c).wait()


def shards(sizes, heads_out, grad_out, error, q_warm):
    ny, nx, nz = sizes
    tokens, m = heads_out.shape
    bk, width = grad_out.shape
    rank = q_warm.shape[1]
    nc = 2 * ny
    w = width // nc
    half = rank // 2
    eighth = half // nx
    hop = nz // 2
    dma = pltpu.SemaphoreType.DMA
    vmem = pltpu.VMEM
    hbm = pl.BlockSpec(memory_space=pl.ANY)
    return pl.pallas_call(
        functools.partial(kernel, sizes),
        out_shape=(
            jax.ShapeDtypeStruct((rank, m), F32),
            jax.ShapeDtypeStruct((1, rank, width // (ny * nx * 2)), F32),
            jax.ShapeDtypeStruct((1, m, width), BF16),
        ),
        in_specs=[hbm] * 4,
        out_specs=(pl.BlockSpec(memory_space=vmem), pl.BlockSpec(memory_space=vmem), hbm),
        scratch_shapes=[
            vmem((nc, bk, w), BF16),
            vmem((2 * (hop - 1) + 1, nc, bk, w), BF16),
            vmem((tokens, m), BF16),
            vmem((nz, m, bk), BF16),
            vmem((nc, m, w), BF16),
            vmem((nc, m, w), F32),
            vmem((nc, rank, w), F32),
            vmem((nc, 2 * rank, w), BF16),
            vmem((2 * rank, tokens), F32),
            vmem((2 * rank, m), F32),
            vmem((rank, m), F32),
            vmem((half, m), F32),
            vmem((nx, half, m), F32),
            vmem((ny, half, m), F32),
            vmem((rank, m), F32),
            vmem((rank, m + 128), F32),
            vmem((nc, rank, w), F32),
            vmem((nc, half, w), F32),
            vmem((nx, ny, eighth, w), F32),
            vmem((ny, eighth, w), F32),
            vmem((ny, eighth, w), F32),
            vmem((ny, half, w), F32),
            vmem((half, w), F32),
            vmem((nx, eighth, w), F32),
            vmem((nc, rank, w), F32),
            vmem((nz, 8, 128), F32),
            dma((4, nc)),
            dma((nc,)),
            dma((2, hop, nc)),
            dma((2, hop, nc)),
            dma((nx + ny + 1,)),
            dma((nx + ny + 1,)),
            dma((8, max(nx, ny))),
            dma((8, max(nx, ny))),
            dma((nc,)),
            dma((nc,)),
            dma((nz,)),
            dma((nz,)),
        ],
        compiler_params=pltpu.CompilerParams(
            collective_id=0, has_side_effects=True, vmem_limit_bytes=58 * 2**20
        ),
    )(heads_out, grad_out, error, q_warm)


def solution(mesh, ny=4, nx=4):
    placed = (
        P("dp", "tensor"),
        P(("dp", "tensor"), None),
        P("dp", "tensor", None),
        P("tensor", None, None),
    )
    return jax.shard_map(
        functools.partial(shards, (ny, nx, mesh.shape["tensor"])),
        mesh=mesh,
        in_specs=placed,
        out_specs=(P(None, "tensor"), P("tensor", None, "dp"), P("dp", "tensor", None)),
        check_vma=False,
    )
```

```python
import functools

import jax
import jax.numpy as jnp
from jax import lax
from jax.experimental import pallas as pl
from jax.experimental.pallas import tpu as pltpu
from jax.sharding import PartitionSpec as P

MESH = pl.DeviceIdType.MESH
F32 = jnp.float32
BF16 = jnp.bfloat16


def split(value):
    high = value.astype(BF16)
    return high, (value - high.astype(F32)).astype(BF16)


def dot(a, b, a_dim, b_dim, **options):
    return lax.dot_general(a, b, (((a_dim,), (b_dim,)), ((), ())), preferred_element_type=F32, **options)


def triple(value):
    first = value.astype(BF16).astype(F32)
    rest = value - first
    second = rest.astype(BF16).astype(F32)
    return first, second, rest - second


def orthonormal(ch, rows, cols):
    place = lax.broadcasted_iota(jnp.int32, (8, 1), 0)
    tiles = range(ch.shape[1] // 128)

    def block(r, carry):
        start = pl.multiple_of(r * 8, 8)
        top = ch[pl.ds(start, 8), :]
        near = pltpu.roll(top[:, cols:], (128 - r * 8) % 128, 1)
        a = [[jnp.broadcast_to(near[i : i + 1, j : j + 1], (8, 128)) if j >= i else None for j in range(8)] for i in range(8)]
        inverse, upper = [], []
        for i in range(8):
            inverse.append(lax.rsqrt(a[i][i]))
            upper.append([a[i][j] * inverse[i] if j > i else None for j in range(8)])
            for j in range(i + 1, 8):
                for n in range(j, 8):
                    a[j][n] = a[j][n] - upper[i][j] * upper[i][n]
        done, result = [], [jnp.zeros((8, 128), F32) for _ in tiles]
        for i in range(8):
            row = [jnp.broadcast_to(top[i : i + 1, t * 128 : t * 128 + 128], (8, 128)) for t in tiles]
            for j in range(i):
                row = [row[t] - upper[j][i] * done[j][t] for t in tiles]
            row = [row[t] * inverse[i] for t in tiles]
            done.append(row)
            result = [jnp.where(place == i, row[t], result[t]) for t in tiles]
        top = jnp.concatenate(result, axis=1)
        ch[pl.ds(start, 8), :] = top
        a1, a2, a3 = triple(top[:, cols : cols + rows])
        b1, b2, b3 = triple(top)
        left = jnp.concatenate([a1, a1, a1, a2, a2, a3], axis=0).astype(BF16)
        right = jnp.concatenate([b1, b2, b3, b1, b2, b1], axis=0).astype(BF16)
        below = lax.broadcasted_iota(jnp.int32, (rows, 1), 0) >= (r + 1) * 8
        ch[...] = jnp.where(below, ch[...] - dot(left, right, 0, 0), ch[...])
        return carry

    lax.fori_loop(0, rows // 8, block, 0)


def kernel(
    sizes, heads, grad, err, q, p_out, q_out, e_out,
    own, gath, hv, at, ev, acc, qv, qs, g, pe, pt, pr, py, pf, ch,
    f, fc, xa, sa, ya, yb, sb, xb, ff, en, eh, qo, gs, gr,
    in_sem, out_sem, ring_send, ring_recv, p_send, p_recv, f_send, f_recv, c_send, c_recv, e_send, e_recv, q_send, q_recv,
):
    ny, nx, nz = sizes
    nc = 2 * ny
    bk, w = own.shape[1], own.shape[2]
    rank = qv.shape[1]
    half = rank // 2
    eighth = half // nx
    hop = nz // 2
    replicas = ny * nx * 2
    k, z = lax.axis_index("dp"), lax.axis_index("tensor")
    core, x, y = k % 2, (k // 2) % nx, k // (2 * nx)

    def at_dp(y_to, x_to, core_to):
        return ((y_to * nx + x_to) * 2 + core_to, z)

    other_core = at_dp(y, x, 1 - core)
    x_peer = [None] + [at_dp(y, (x + d) % nx, core) for d in range(1, nx)]
    y_peer = [None] + [at_dp((y + d) % ny, x, core) for d in range(1, ny)]
    row_len = 2 * nx
    row_at = x * 2 + core
    row_of = [(row_at + d) % row_len for d in range(row_len)]
    row_peer = [None] + [at_dp(y, row_of[d] // 2, row_of[d] % 2) for d in range(1, row_len)]
    z_peer = [None] + [(k, (z + d) % nz) for d in range(1, nz)]

    def remote(src, dst, send, recv, device):
        return pltpu.make_async_remote_copy(
            src_ref=src, dst_ref=dst, send_sem=send, recv_sem=recv, device_id=device, device_id_type=MESH
        )

    def loop(begin, end):
        def run(body):
            def step(c, carry):
                body(c)
                return carry

            lax.fori_loop(begin, end, step, 0)

        return run

    chunk_loop = loop(0, nc)
    window = min(4, nc // 2)

    def cols(c):
        return pl.ds(pl.multiple_of(c * w, w), w)

    def load_own(c):
        return pltpu.make_async_copy(grad.at[:, cols(c)], own.at[c], in_sem.at[0, c])

    def load_err(c):
        return pltpu.make_async_copy(err.at[0, :, cols(c)], ev.at[c], in_sem.at[1, c])

    def load_q(c):
        return pltpu.make_async_copy(q.at[0, :, cols(c)], qv.at[c], in_sem.at[2, c])

    load_heads = pltpu.make_async_copy(heads, hv, in_sem.at[3, 0])

    barrier = pltpu.get_barrier_semaphore()
    everyone = row_peer[1:] + y_peer[1:] + z_peer[1:]
    for device in everyone:
        pl.semaphore_signal(barrier, inc=1, device_id=device, device_id_type=MESH)

    load_heads.start()

    @chunk_loop
    def _(c):
        load_own(c).start()
        load_q(c).start()
        load_err(c).start()

    pl.semaphore_wait(barrier, len(everyone))

    far = 2 * (hop - 1)

    def slot(way, s):
        return way * (hop - 1) + s - 1

    def ring(way, s, c):
        part = pl.ds(way * (bk // 2), bk // 2)
        if s == 0:
            src = grad.at[:, cols(c)]
        else:
            src = gath.at[slot(way, s), c]
        if s == hop - 1:
            if s == 0:
                src = grad.at[part, cols(c)]
            else:
                src = gath.at[slot(way, s), c, part]
            dst = gath.at[far, c, part]
        else:
            dst = gath.at[slot(way, s + 1), c]
        return remote(src, dst, ring_send.at[way, s, c], ring_recv.at[way, s, c], z_peer[1] if way == 0 else z_peer[nz - 1])

    mine = pl.ds(pl.multiple_of(core * half, half), half)
    theirs = pl.ds(pl.multiple_of((1 - core) * half, half), half)

    per_chunk = nx // 2
    q_width = 2 * w // nx
    q_piece = pl.ds(pl.multiple_of((y * nx + x) * q_width, q_width), q_width)
    q_place = (2 * y + x // per_chunk, mine, pl.ds(pl.multiple_of((x % per_chunk) * q_width, q_width), q_width))
    opposite = z_peer[hop]

    def q_spread(place, first, peers):
        return [
            remote(qo.at[place], qo.at[place], q_send.at[first + d], q_recv.at[first + d], peers[d])
            for d in range(1, len(peers))
        ]

    q_over_z = remote(q.at[0, mine, q_piece], qo.at[q_place], q_send.at[0], q_recv.at[0], opposite)
    q_over_x = q_spread(q_place, 0, x_peer)
    q_over_y = q_spread((pl.ds(2 * y, 2), mine), nx - 1, y_peer)
    q_over_core = q_spread((pl.ds(0, nc), mine), nx + ny - 2, [None, other_core])
    g_over_z = remote(gs, gr, q_send.at[nx + ny], q_recv.at[nx + ny], opposite)

    q_over_z.start()

    @loop(0, window)
    def _(c):
        ring(0, 0, c).start()
        ring(1, 0, c).start()

    load_heads.wait()

    def flip(i, carry):
        at[i] = hv[pl.ds(pl.multiple_of(i * bk, bk), bk), :].astype(F32).T.astype(BF16)
        return carry

    lax.fori_loop(0, nz, flip, 0)
    g[...] = jnp.zeros_like(g)
    pe[...] = jnp.zeros_like(pe)

    def use(block, c, which):
        acc[c] += dot(at[which], block, 1, 0)

    def use_both(block, c, which):
        use(block, c, which)
        place = pl.ds(pl.multiple_of(which * bk, bk), bk)
        g[:, place] += dot(qs[c], block, 1, 1)

    def own_chunk(c):
        load_q(c).wait()
        high, low = split(qv[c])
        qs[c, 0:rank, :] = high
        qs[c, rank:, :] = low
        load_err(c).wait()
        acc[c] = ev[c].astype(F32)
        pe[...] += dot(qs[c], ev[c], 1, 1)
        load_own(c).wait()
        use_both(own[c], c, z)

    @loop(0, nc - window)
    def _(c):
        own_chunk(c)
        for way in range(2):
            ring(way, 0, c).wait_send()
            ring(way, 0, c + window).start()

    loop(nc - window, nc)(own_chunk)

    def q_step_x():
        q_over_z.wait()
        for copy in q_over_x:
            copy.start()

    def q_step_y():
        for copy in q_over_x:
            copy.wait()
        for copy in q_over_y:
            copy.start()

    def q_step_core():
        for copy in q_over_y:
            copy.wait()
        for copy in q_over_core:
            copy.start()
        for copy in q_over_core:
            copy.wait()

        def term(c, total):
            high, low = split(qo[c])
            return total + dot(jnp.concatenate([high, low], axis=0), own[c], 1, 1)

        total = lax.fori_loop(0, nc, term, jnp.zeros((2 * rank, bk), F32))
        gs[...] = total[0:rank] + total[rank:]
        g_over_z.start()

    q_step_x()
    steps = [q_step_y, q_step_core]

    def ring_chunk(s, before):
        def run(c):
            for way in range(2):
                ring(way, s - 1, c).wait_recv()
                if before is not None:
                    ring(way, *before(c)).wait_send()
                ring(way, s, c).start()
            use_both(gath[slot(0, s), c], c, (z - s + nz) % nz)
            use_both(gath[slot(1, s), c], c, (z + s) % nz)

        return run

    for s in range(1, hop):
        if s < hop - 1:
            loop(0, window)(ring_chunk(s, lambda c: (s - 1, nc - window + c)))
            loop(window, nc)(ring_chunk(s, lambda c: (s, c - window)))
        else:
            chunk_loop(ring_chunk(s, None))
        if steps:
            steps.pop(0)()
    for step in steps:
        step()
    g_over_z.wait()
    g[0:rank, pl.ds(pl.multiple_of(((z + hop) % nz) * bk, bk), bk)] = gr[...]

    def rows_of(core_at, x_at):
        return pl.ds(pl.multiple_of(core_at * half + x_at * eighth, eighth), eighth)

    rows = rows_of(core, x)

    def run_all(copies):
        for copy in copies:
            copy.start()
        for copy in copies:
            copy.wait()

    def total_of(ref, count):
        return functools.reduce(lambda a, b: a + b, [ref[i] for i in range(count)])

    total = g[0:rank, :] + g[rank:, :]
    high, low = split(total)
    terms = dot(jnp.concatenate([high, low], axis=0), hv[...], 1, 0) + pe[...]
    pt[...] = terms[0:rank, :] + terms[rank:, :]
    pr[row_at] = pt[rows, :]
    run_all([
        remote(pt.at[rows_of(row_of[d] % 2, row_of[d] // 2)], pr.at[row_at], p_send.at[0, d], p_recv.at[0, d], row_peer[d])
        for d in range(1, row_len)
    ])
    py[y] = total_of(pr, row_len)
    run_all([remote(py.at[y], py.at[y], p_send.at[1, d], p_recv.at[1, d], y_peer[d]) for d in range(1, ny)])
    pf[rows, :] = total_of(py, ny)
    run_all([remote(pf.at[rows], pf.at[rows], p_send.at[2, d], p_recv.at[2, d], row_peer[d]) for d in range(1, row_len)])

    m = pf.shape[1]
    ch[:, 0:m] = pf[...]
    ch[:, m:] = jnp.zeros((rank, 128), F32)
    ch[:, m : m + rank] = dot(pf[...], pf[...], 1, 1, precision=lax.Precision.HIGHEST)
    orthonormal(ch, rank, m)
    basis = ch[:, 0:m]
    p_out[...] = basis
    b_high, b_low = split(basis)
    b_both = jnp.concatenate([b_high, b_low], axis=0)

    per = ny // 2
    y_width = w // per
    groups = nc // 2

    def in_chunk(c):
        return pl.ds(c * per, per)

    def core_copy(c):
        return remote(f.at[in_chunk(c), theirs], fc.at[in_chunk(c)], c_send.at[c], c_recv.at[c], other_core)

    def factor_chunk(c):
        ring(0, hop - 1, c).wait_recv()
        ring(1, hop - 1, c).wait_recv()
        use(gath[far, c], c, (z + hop) % nz)
        high, low = split(acc[c])
        both = dot(b_both, high, 1, 0)
        both = (both[0:rank] + both[rank:] + dot(b_high, low, 1, 0)) * (1.0 / replicas)
        for i in range(per):
            f[c * per + i] = both[:, i * y_width : (i + 1) * y_width]
        core_copy(c).start()

    def spread(place, i, stage, peers):
        return [
            remote(ff.at[place], ff.at[place], f_send.at[i, stage, d], f_recv.at[i, stage, d], peers[d])
            for d in range(1, len(peers))
        ]

    class Group:
        def __init__(self, i):
            self.i = i
            self.base = i * ny
            self.whole = pl.ds(i * ny, ny)

        def first(self):
            i = self.i

            @loop(2 * i, 2 * i + 2)
            def _(c):
                core_copy(c).wait()

            f[self.whole, mine, :] += fc[self.whole]
            if i % 2 == 0:
                xa[i // 2, x] = f[self.whole, rows, :]
                self.copies = [
                    remote(f.at[self.whole, rows_of(core, (x + d) % nx)], xa.at[i // 2, x], f_send.at[i, 0, d], f_recv.at[i, 0, d], x_peer[d])
                    for d in range(1, nx)
                ]
            else:
                yb[i // 2, y] = f[self.base + y, mine, :]
                self.copies = [
                    remote(f.at[self.base + (y + d) % ny, mine], yb.at[i // 2, y], f_send.at[i, 0, d], f_recv.at[i, 0, d], y_peer[d])
                    for d in range(1, ny)
                ]
            self.start()

        def second(self):
            self.wait()
            i = self.i
            if i % 2 == 0:
                sa[i // 2] = total_of(xa.at[i // 2], nx)
                ya[i // 2, y] = sa[i // 2, y]
                self.copies = [
                    remote(sa.at[i // 2, (y + d) % ny], ya.at[i // 2, y], f_send.at[i, 1, d], f_recv.at[i, 1, d], y_peer[d])
                    for d in range(1, ny)
                ]
            else:
                sb[i // 2] = total_of(yb.at[i // 2], ny)

                def part(x_at):
                    return pl.ds(pl.multiple_of(x_at * eighth, eighth), eighth)

                xb[i // 2, x] = sb[i // 2, part(x), :]
                self.copies = [
                    remote(sb.at[i // 2, part((x + d) % nx)], xb.at[i // 2, x], f_send.at[i, 1, d], f_recv.at[i, 1, d], x_peer[d])
                    for d in range(1, nx)
                ]
            self.start()

        def third(self):
            self.wait()
            if self.i % 2 == 0:
                ff[self.base + y, rows, :] = total_of(ya.at[self.i // 2], ny)
            else:
                ff[self.base + y, rows, :] = total_of(xb.at[self.i // 2], nx)
            self.copies = spread((self.base + y, rows), self.i, 2, y_peer if self.i % 2 == 0 else x_peer)
            self.start()

        def fourth(self):
            self.wait()
            if self.i % 2 == 0:
                self.copies = spread((self.whole, rows), self.i, 3, x_peer)
            else:
                self.copies = spread((self.base + y, mine), self.i, 3, y_peer)
            self.start()

        def fifth(self):
            self.wait()
            self.copies = spread((self.whole, mine), self.i, 4, [None, other_core])
            self.start()

        def start(self):
            for copy in self.copies:
                copy.start()

        def wait(self):
            for copy in self.copies:
                copy.wait()

    every = [Group(i) for i in range(groups)]
    for group in every:
        loop(2 * group.i, 2 * group.i + 2)(factor_chunk)
        if group.i > 0:
            every[group.i - 1].first()
    every[-1].first()
    for step in ("second", "third", "fourth", "fifth"):
        for group in every:
            getattr(group, step)()

    def squares(i, carry):
        value = ff[i, mine, :]
        return carry + jnp.sum(value * value, axis=(0, 1), keepdims=True)

    energy = lax.fori_loop(0, nc * per, squares, jnp.zeros((1, 1), F32))
    en[z] = jnp.broadcast_to(energy, (8, 128))
    energies = [remote(en.at[z], en.at[z], e_send.at[d], e_recv.at[d], z_peer[d]) for d in range(1, nz)]
    for copy in energies:
        copy.start()

    b_wide = jnp.concatenate([b_high, b_high, b_low], axis=0).astype(F32).T.astype(BF16)

    def store(c):
        return pltpu.make_async_copy(ev.at[c], e_out.at[0, :, cols(c)], out_sem.at[c])

    def last_chunk(c):
        high, low = split(jnp.concatenate([ff[c * per + i] for i in range(per)], axis=1))
        approx = dot(b_wide, jnp.concatenate([high, low, high], axis=0), 1, 0)
        ev[c] = (acc[c] - approx).astype(BF16)
        store(c).start()

    for group in every:
        group.wait()
        loop(2 * group.i, 2 * group.i + 2)(last_chunk)

    for copy in energies:
        copy.wait()
    eh[core] = total_of(en, nz)
    run_all([remote(eh.at[core], eh.at[core], e_send.at[0], e_recv.at[0], other_core)])
    entire = (eh[0] + eh[1])[0:1, 0:1]
    scale = lax.rsqrt(entire * (1.0 / (m * nz * w * nc)) + 1e-06)
    width = q_out.shape[2]
    ahead = y_width // width
    piece = ff[k // ahead]
    piece = pltpu.roll(piece, (y_width - (k % ahead) * width) % y_width, 1)
    q_out[0] = piece[:, 0:width] * scale

    @loop(nc - window, nc)
    def _(c):
        ring(0, hop - 2, c).wait_send()
        ring(1, hop - 2, c).wait_send()

    @chunk_loop
    def _(c):
        ring(0, hop - 1, c).wait_send()
        ring(1, hop - 1, c).wait_send()

    @chunk_loop
    def _(c):
        store(c).wait()


def hand_over(p, q, e, p_out, q_out, e_out, p_held, q_held, e_held, come, go):
    parts = go.shape[0] - 2
    rows = e_held.shape[1] // parts

    def part(i):
        return (0, pl.ds(i * rows, rows))

    pairs = [(p, p_held, p_out), (q, q_held, q_out)]
    pairs += [(e.at[part(i)], e_held.at[part(i)], e_out.at[part(i)]) for i in range(parts)]
    ins = [pltpu.make_async_copy(src, held, come.at[i]) for i, (src, held, _) in enumerate(pairs)]
    outs = [pltpu.make_async_copy(held, dst, go.at[i]) for i, (_, held, dst) in enumerate(pairs)]
    for copy in ins:
        copy.start()
    for copy, onward in zip(ins, outs):
        copy.wait()
        onward.start()
    for copy in outs:
        copy.wait()


def shards(sizes, heads_out, grad_out, error, q_warm):
    ny, nx, nz = sizes
    tokens, m = heads_out.shape
    bk, width = grad_out.shape
    rank = q_warm.shape[1]
    nc = 2 * ny
    w = width // nc
    half = rank // 2
    eighth = half // nx
    hop = nz // 2
    y_width = 2 * w // ny
    count = nc * ny // 2
    pairs = (ny + 1) // 2
    dma = pltpu.SemaphoreType.DMA
    vmem = pltpu.VMEM
    hbm = pl.BlockSpec(memory_space=pl.ANY)
    outs = (
        jax.ShapeDtypeStruct((rank, m), F32),
        jax.ShapeDtypeStruct((1, rank, width // (ny * nx * 2)), F32),
        jax.ShapeDtypeStruct((1, m, width), BF16),
    )
    results = pl.pallas_call(
        functools.partial(kernel, sizes),
        out_shape=outs,
        in_specs=[hbm] * 4,
        out_specs=(pl.BlockSpec(memory_space=vmem), pl.BlockSpec(memory_space=vmem), hbm),
        scratch_shapes=[
            vmem((nc, bk, w), BF16),
            vmem((2 * (hop - 1) + 1, nc, bk, w), BF16),
            vmem((tokens, m), BF16),
            vmem((nz, m, bk), BF16),
            vmem((nc, m, w), BF16),
            vmem((nc, m, w), F32),
            vmem((nc, rank, w), F32),
            vmem((nc, 2 * rank, w), BF16),
            vmem((2 * rank, tokens), F32),
            vmem((2 * rank, m), F32),
            vmem((rank, m), F32),
            vmem((2 * nx, eighth, m), F32),
            vmem((ny, eighth, m), F32),
            vmem((rank, m), F32),
            vmem((rank, m + 128), F32),
            vmem((count, rank, y_width), F32),
            vmem((count, half, y_width), F32),
            vmem((pairs, nx, ny, eighth, y_width), F32),
            vmem((pairs, ny, eighth, y_width), F32),
            vmem((pairs, ny, eighth, y_width), F32),
            vmem((pairs, ny, half, y_width), F32),
            vmem((pairs, half, y_width), F32),
            vmem((pairs, nx, eighth, y_width), F32),
            vmem((count, rank, y_width), F32),
            vmem((nz, 8, 128), F32),
            vmem((2, 8, 128), F32),
            vmem((nc, rank, w), F32),
            vmem((rank, bk), F32),
            vmem((rank, bk), F32),
            dma((4, nc)),
            dma((nc,)),
            dma((2, hop, nc)),
            dma((2, hop, nc)),
            dma((3, max(2 * nx, ny))),
            dma((3, max(2 * nx, ny))),
            dma((nc // 2, 5, max(nx, ny))),
            dma((nc // 2, 5, max(nx, ny))),
            dma((nc,)),
            dma((nc,)),
            dma((nz,)),
            dma((nz,)),
            dma((nx + ny + 1,)),
            dma((nx + ny + 1,)),
        ],
        compiler_params=pltpu.CompilerParams(
            collective_id=0, has_side_effects=True, vmem_limit_bytes=58 * 2**20
        ),
    )(heads_out, grad_out, error, q_warm)
    parts = 6 if m % 96 == 0 else 4
    return pl.pallas_call(
        hand_over,
        out_shape=outs,
        in_specs=[hbm] * 3,
        out_specs=(hbm,) * 3,
        scratch_shapes=[vmem(out.shape, out.dtype) for out in outs] + [dma((parts + 2,)), dma((parts + 2,))],
        compiler_params=pltpu.CompilerParams(vmem_limit_bytes=60 * 2**20),
    )(*results)


def solution(mesh, ny=4, nx=4):
    placed = (
        P("dp", "tensor"),
        P(("dp", "tensor"), None),
        P("dp", "tensor", None),
        P("tensor", None, None),
    )
    return jax.shard_map(
        functools.partial(shards, (ny, nx, mesh.shape["tensor"])),
        mesh=mesh,
        in_specs=placed,
        out_specs=(P(None, "tensor"), P("tensor", None, "dp"), P("dp", "tensor", None)),
        check_vma=False,
    )
```

```python
import functools

import jax
import jax.numpy as jnp
from jax import lax
from jax.experimental import pallas as pl
from jax.experimental.pallas import tpu as pltpu
from jax.sharding import PartitionSpec as P

MESH = pl.DeviceIdType.MESH
F32 = jnp.float32
BF16 = jnp.bfloat16


def split(value):
    high = value.astype(BF16)
    return high, (value - high.astype(F32)).astype(BF16)


def dot(a, b, a_dim, b_dim, **options):
    return lax.dot_general(a, b, (((a_dim,), (b_dim,)), ((), ())), preferred_element_type=F32, **options)


def triple(value):
    first = value.astype(BF16).astype(F32)
    rest = value - first
    second = rest.astype(BF16).astype(F32)
    return first, second, rest - second


def orthonormal(ch, rows, cols):
    place = lax.broadcasted_iota(jnp.int32, (8, 1), 0)
    tiles = range(ch.shape[1] // 128)

    def block(r, carry):
        start = pl.multiple_of(r * 8, 8)
        top = ch[pl.ds(start, 8), :]
        near = pltpu.roll(top[:, cols:], (128 - r * 8) % 128, 1)
        a = [[jnp.broadcast_to(near[i : i + 1, j : j + 1], (8, 128)) if j >= i else None for j in range(8)] for i in range(8)]
        inverse, upper = [], []
        for i in range(8):
            inverse.append(lax.rsqrt(a[i][i]))
            upper.append([a[i][j] * inverse[i] if j > i else None for j in range(8)])
            for j in range(i + 1, 8):
                for n in range(j, 8):
                    a[j][n] = a[j][n] - upper[i][j] * upper[i][n]
        done, result = [], [jnp.zeros((8, 128), F32) for _ in tiles]
        for i in range(8):
            row = [jnp.broadcast_to(top[i : i + 1, t * 128 : t * 128 + 128], (8, 128)) for t in tiles]
            for j in range(i):
                row = [row[t] - upper[j][i] * done[j][t] for t in tiles]
            row = [row[t] * inverse[i] for t in tiles]
            done.append(row)
            result = [jnp.where(place == i, row[t], result[t]) for t in tiles]
        top = jnp.concatenate(result, axis=1)
        ch[pl.ds(start, 8), :] = top
        a1, a2, a3 = triple(top[:, cols : cols + rows])
        b1, b2, b3 = triple(top)
        left = jnp.concatenate([a1, a1, a1, a2, a2, a3], axis=0).astype(BF16)
        right = jnp.concatenate([b1, b2, b3, b1, b2, b1], axis=0).astype(BF16)
        below = lax.broadcasted_iota(jnp.int32, (rows, 1), 0) >= (r + 1) * 8
        ch[...] = jnp.where(below, ch[...] - dot(left, right, 0, 0), ch[...])
        return carry

    lax.fori_loop(0, rows // 8, block, 0)


def kernel(
    sizes, heads, grad, err, q, p_out, q_out, e_out,
    own, gath, hv, at, ev, acc, qv, qs, g, pe, pt, pr, py, pf, ch,
    f, fc, xa, sa, yb, sb, ff, en, eh, qo, gs, gr,
    in_sem, out_sem, ring_send, ring_recv, p_send, p_recv, f_send, f_recv, c_send, c_recv, e_send, e_recv, q_send, q_recv,
):
    ny, nx, nz = sizes
    nc = 2 * ny
    bk, w = own.shape[1], own.shape[2]
    rank = qv.shape[1]
    half = rank // 2
    eighth = half // nx
    hop = nz // 2
    replicas = ny * nx * 2
    k, z = lax.axis_index("dp"), lax.axis_index("tensor")
    core, x, y = k % 2, (k // 2) % nx, k // (2 * nx)

    def at_dp(y_to, x_to, core_to):
        return ((y_to * nx + x_to) * 2 + core_to, z)

    other_core = at_dp(y, x, 1 - core)
    x_peer = [None] + [at_dp(y, (x + d) % nx, core) for d in range(1, nx)]
    y_peer = [None] + [at_dp((y + d) % ny, x, core) for d in range(1, ny)]
    row_len = 2 * nx
    row_at = x * 2 + core
    row_of = [(row_at + d) % row_len for d in range(row_len)]
    row_peer = [None] + [at_dp(y, row_of[d] // 2, row_of[d] % 2) for d in range(1, row_len)]
    z_peer = [None] + [(k, (z + d) % nz) for d in range(1, nz)]

    def remote(src, dst, send, recv, device):
        return pltpu.make_async_remote_copy(
            src_ref=src, dst_ref=dst, send_sem=send, recv_sem=recv, device_id=device, device_id_type=MESH
        )

    def loop(begin, end):
        def run(body):
            def step(c, carry):
                body(c)
                return carry

            lax.fori_loop(begin, end, step, 0)

        return run

    chunk_loop = loop(0, nc)
    window = min(4, nc // 2)

    def cols(c):
        return pl.ds(pl.multiple_of(c * w, w), w)

    def load_own(c):
        return pltpu.make_async_copy(grad.at[:, cols(c)], own.at[c], in_sem.at[0, c])

    def load_err(c):
        return pltpu.make_async_copy(err.at[0, :, cols(c)], ev.at[c], in_sem.at[1, c])

    def load_q(c):
        return pltpu.make_async_copy(q.at[0, :, cols(c)], qv.at[c], in_sem.at[2, c])

    load_heads = pltpu.make_async_copy(heads, hv, in_sem.at[3, 0])

    barrier = pltpu.get_barrier_semaphore()
    everyone = row_peer[1:] + y_peer[1:] + z_peer[1:]
    for device in everyone:
        pl.semaphore_signal(barrier, inc=1, device_id=device, device_id_type=MESH)

    load_heads.start()

    @chunk_loop
    def _(c):
        load_own(c).start()
        load_q(c).start()
        load_err(c).start()

    pl.semaphore_wait(barrier, len(everyone))

    far = 2 * (hop - 1)

    def slot(way, s):
        return way * (hop - 1) + s - 1

    def ring(way, s, c):
        part = pl.ds(way * (bk // 2), bk // 2)
        if s == 0:
            src = grad.at[:, cols(c)]
        else:
            src = gath.at[slot(way, s), c]
        if s == hop - 1:
            if s == 0:
                src = grad.at[part, cols(c)]
            else:
                src = gath.at[slot(way, s), c, part]
            dst = gath.at[far, c, part]
        else:
            dst = gath.at[slot(way, s + 1), c]
        return remote(src, dst, ring_send.at[way, s, c], ring_recv.at[way, s, c], z_peer[1] if way == 0 else z_peer[nz - 1])

    mine = pl.ds(pl.multiple_of(core * half, half), half)
    theirs = pl.ds(pl.multiple_of((1 - core) * half, half), half)

    per_chunk = nx // 2
    q_width = 2 * w // nx
    q_piece = pl.ds(pl.multiple_of((y * nx + x) * q_width, q_width), q_width)
    q_place = (2 * y + x // per_chunk, mine, pl.ds(pl.multiple_of((x % per_chunk) * q_width, q_width), q_width))
    opposite = z_peer[hop]

    def q_spread(place, first, peers):
        return [
            remote(qo.at[place], qo.at[place], q_send.at[first + d], q_recv.at[first + d], peers[d])
            for d in range(1, len(peers))
        ]

    q_over_z = remote(q.at[0, mine, q_piece], qo.at[q_place], q_send.at[0], q_recv.at[0], opposite)
    q_over_x = q_spread(q_place, 0, x_peer)
    q_over_y = q_spread((pl.ds(2 * y, 2), mine), nx - 1, y_peer)
    q_over_core = q_spread((pl.ds(0, nc), mine), nx + ny - 2, [None, other_core])
    g_over_z = remote(gs, gr, q_send.at[nx + ny], q_recv.at[nx + ny], opposite)

    q_over_z.start()

    @loop(0, window)
    def _(c):
        ring(0, 0, c).start()
        ring(1, 0, c).start()

    load_heads.wait()

    def flip(i, carry):
        at[i] = hv[pl.ds(pl.multiple_of(i * bk, bk), bk), :].astype(F32).T.astype(BF16)
        return carry

    lax.fori_loop(0, nz, flip, 0)
    g[...] = jnp.zeros_like(g)
    pe[...] = jnp.zeros_like(pe)

    def use(block, c, which):
        acc[c] += dot(at[which], block, 1, 0)

    def use_both(block, c, which):
        use(block, c, which)
        place = pl.ds(pl.multiple_of(which * bk, bk), bk)
        g[:, place] += dot(qs[c], block, 1, 1)

    def own_chunk(c):
        load_q(c).wait()
        high, low = split(qv[c])
        qs[c, 0:rank, :] = high
        qs[c, rank:, :] = low
        load_err(c).wait()
        acc[c] = ev[c].astype(F32)
        pe[...] += dot(qs[c], ev[c], 1, 1)
        load_own(c).wait()
        use_both(own[c], c, z)

    @loop(0, nc - window)
    def _(c):
        own_chunk(c)
        for way in range(2):
            ring(way, 0, c).wait_send()
            ring(way, 0, c + window).start()

    loop(nc - window, nc)(own_chunk)

    def q_step_x():
        q_over_z.wait()
        for copy in q_over_x:
            copy.start()

    def q_step_y():
        for copy in q_over_x:
            copy.wait()
        for copy in q_over_y:
            copy.start()

    def q_step_core():
        for copy in q_over_y:
            copy.wait()
        for copy in q_over_core:
            copy.start()
        for copy in q_over_core:
            copy.wait()

        def term(c, total):
            high, low = split(qo[c])
            return total + dot(jnp.concatenate([high, low], axis=0), own[c], 1, 1)

        total = lax.fori_loop(0, nc, term, jnp.zeros((2 * rank, bk), F32))
        gs[...] = total[0:rank] + total[rank:]
        g_over_z.start()

    q_step_x()
    steps = [q_step_y, q_step_core]

    def ring_chunk(s, before, begin=0, end=0):
        def run(c):
            for way in range(2):
                ring(way, s - 1, c).wait_recv()
                if before is not None:
                    ring(way, *before(c)).wait_send()
                    ring(way, s, c).start()
            for other in range(begin, end):
                ring(0, s, other).start()
                ring(1, s, other).start()
            use_both(gath[slot(0, s), c], c, (z - s + nz) % nz)
            use_both(gath[slot(1, s), c], c, (z + s) % nz)

        return run

    for s in range(1, hop):
        if s < hop - 1:
            loop(0, window)(ring_chunk(s, lambda c: (s - 1, nc - window + c)))
            loop(window, nc)(ring_chunk(s, lambda c: (s, c - window)))
        else:
            late = min(3, nc - 1)
            loop(0, nc - late)(ring_chunk(s, None))
            for i in range(late):
                ring_chunk(s, None, i * nc // 4, (i + 1) * nc // 4 if i < late - 1 else nc)(nc - late + i)
        if steps:
            steps.pop(0)()
    for step in steps:
        step()
    g_over_z.wait()
    g[0:rank, pl.ds(pl.multiple_of(((z + hop) % nz) * bk, bk), bk)] = gr[...]

    def rows_of(core_at, x_at):
        return pl.ds(pl.multiple_of(core_at * half + x_at * eighth, eighth), eighth)

    rows = rows_of(core, x)

    def run_all(copies):
        for copy in copies:
            copy.start()
        for copy in copies:
            copy.wait()

    def total_of(ref, count):
        return functools.reduce(lambda a, b: a + b, [ref[i] for i in range(count)])

    total = g[0:rank, :] + g[rank:, :]
    high, low = split(total)
    terms = dot(jnp.concatenate([high, low], axis=0), hv[...], 1, 0) + pe[...]
    pt[...] = terms[0:rank, :] + terms[rank:, :]
    pr[row_at] = pt[rows, :]
    run_all([
        remote(pt.at[rows_of(row_of[d] % 2, row_of[d] // 2)], pr.at[row_at], p_send.at[0, d], p_recv.at[0, d], row_peer[d])
        for d in range(1, row_len)
    ])
    py[y] = total_of(pr, row_len)
    run_all([remote(py.at[y], py.at[y], p_send.at[1, d], p_recv.at[1, d], y_peer[d]) for d in range(1, ny)])
    pf[rows, :] = total_of(py, ny)
    run_all([remote(pf.at[rows], pf.at[rows], p_send.at[2, d], p_recv.at[2, d], row_peer[d]) for d in range(1, row_len)])

    m = pf.shape[1]
    ch[:, 0:m] = pf[...]
    ch[:, m:] = jnp.zeros((rank, 128), F32)
    ch[:, m : m + rank] = dot(pf[...], pf[...], 1, 1, precision=lax.Precision.HIGHEST)
    orthonormal(ch, rank, m)
    basis = ch[:, 0:m]
    basis_out = pltpu.make_async_copy(ch.at[:, pl.ds(0, m)], p_out, in_sem.at[3, 1])
    basis_out.start()
    b_high, b_low = split(basis)
    b_both = jnp.concatenate([b_high, b_low], axis=0)

    per = ny // 2
    y_width = w // per
    groups = nc // 2

    def in_chunk(c):
        return pl.ds(c * per, per)

    def core_copy(c):
        return remote(f.at[in_chunk(c), theirs], fc.at[in_chunk(c)], c_send.at[c], c_recv.at[c], other_core)

    def factor_chunk(c):
        ring(0, hop - 1, c).wait_recv()
        ring(1, hop - 1, c).wait_recv()
        use(gath[far, c], c, (z + hop) % nz)
        high, low = split(acc[c])
        both = dot(b_both, high, 1, 0)
        both = (both[0:rank] + both[rank:] + dot(b_high, low, 1, 0)) * (1.0 / replicas)
        for i in range(per):
            f[c * per + i] = both[:, i * y_width : (i + 1) * y_width]
        core_copy(c).start()

    def spread(place, i, stage, peers):
        return [
            remote(ff.at[place], ff.at[place], f_send.at[i, stage, d], f_recv.at[i, stage, d], peers[d])
            for d in range(1, len(peers))
        ]

    class Group:
        def __init__(self, i):
            self.i = i
            self.base = i * ny
            self.whole = pl.ds(i * ny, ny)

        def first(self):
            i = self.i

            @loop(2 * i, 2 * i + 2)
            def _(c):
                core_copy(c).wait()

            f[self.whole, mine, :] += fc[self.whole]
            if i % 2 == 0:
                xa[i // 2, x] = f[self.whole, rows, :]
                self.copies = [
                    remote(f.at[self.whole, rows_of(core, (x + d) % nx)], xa.at[i // 2, x], f_send.at[i, 0, d], f_recv.at[i, 0, d], x_peer[d])
                    for d in range(1, nx)
                ]
            else:
                yb[i // 2, y] = f[self.base + y, mine, :]
                self.copies = [
                    remote(f.at[self.base + (y + d) % ny, mine], yb.at[i // 2, y], f_send.at[i, 0, d], f_recv.at[i, 0, d], y_peer[d])
                    for d in range(1, ny)
                ]
            self.start()

        def second(self):
            self.wait()
            i = self.i
            if i % 2 == 0:
                sa[i // 2, y] = total_of(xa.at[i // 2], nx)
                mine_now, peers = sa.at[i // 2, y], y_peer
            else:
                sb[i // 2, x] = total_of(yb.at[i // 2], ny)
                mine_now, peers = sb.at[i // 2, x], x_peer
            self.copies = [
                remote(mine_now, mine_now, f_send.at[i, 1, d], f_recv.at[i, 1, d], peers[d]) for d in range(1, len(peers))
            ]
            self.start()

        def third(self):
            self.wait()
            i = self.i
            if i % 2 == 0:
                ff[self.whole, rows, :] = total_of(sa.at[i // 2], ny)
                self.copies = spread((self.whole, rows), i, 2, x_peer)
            else:
                ff[self.base + y, mine, :] = total_of(sb.at[i // 2], nx)
                self.copies = spread((self.base + y, mine), i, 2, y_peer)
            self.start()

        def fourth(self):
            self.wait()
            self.copies = spread((self.whole, mine), self.i, 3, [None, other_core])
            self.start()

        def start(self):
            for copy in self.copies:
                copy.start()

        def wait(self):
            for copy in self.copies:
                copy.wait()

    every = [Group(i) for i in range(groups)]
    for group in every:
        loop(2 * group.i, 2 * group.i + 2)(factor_chunk)
        if group.i > 0:
            every[group.i - 1].first()
    every[-1].first()
    for step in ("second", "third", "fourth"):
        for group in every:
            getattr(group, step)()

    def squares(i, carry):
        value = ff[i, mine, :]
        return carry + jnp.sum(value * value, axis=(0, 1), keepdims=True)

    energy = lax.fori_loop(0, nc * per, squares, jnp.zeros((1, 1), F32))
    en[z] = jnp.broadcast_to(energy, (8, 128))
    energies = [remote(en.at[z], en.at[z], e_send.at[d], e_recv.at[d], z_peer[d]) for d in range(1, nz)]
    for copy in energies:
        copy.start()

    b_wide = jnp.concatenate([b_high, b_high, b_low], axis=0).astype(F32).T.astype(BF16)

    def store(c):
        return pltpu.make_async_copy(ev.at[c], e_out.at[0, :, cols(c)], out_sem.at[c])

    def last_chunk(c):
        high, low = split(jnp.concatenate([ff[c * per + i] for i in range(per)], axis=1))
        approx = dot(b_wide, jnp.concatenate([high, low, high], axis=0), 1, 0)
        ev[c] = (acc[c] - approx).astype(BF16)
        store(c).start()

    over_core = remote(eh.at[core], eh.at[core], e_send.at[0], e_recv.at[0], other_core)
    for group in every:
        group.wait()
        if group is every[-1]:
            for copy in energies:
                copy.wait()
            eh[core] = total_of(en, nz)
            over_core.start()
        loop(2 * group.i, 2 * group.i + 2)(last_chunk)
    over_core.wait()
    entire = (eh[0] + eh[1])[0:1, 0:1]
    scale = lax.rsqrt(entire * (1.0 / (m * nz * w * nc)) + 1e-06)
    width = q_out.shape[2]
    ahead = y_width // width
    piece = ff[k // ahead]
    piece = pltpu.roll(piece, (y_width - (k % ahead) * width) % y_width, 1)
    q_out[0] = piece[:, 0:width] * scale

    @loop(nc - window, nc)
    def _(c):
        ring(0, hop - 2, c).wait_send()
        ring(1, hop - 2, c).wait_send()

    @chunk_loop
    def _(c):
        ring(0, hop - 1, c).wait_send()
        ring(1, hop - 1, c).wait_send()

    @chunk_loop
    def _(c):
        store(c).wait()

    basis_out.wait()


def hand_over(p, q, e, p_out, q_out, e_out, p_held, q_held, e_held, come, go):
    parts = go.shape[0] - 2
    rows = e_held.shape[1] // parts

    def part(i):
        return (0, pl.ds(i * rows, rows))

    pairs = [(p, p_held, p_out), (q, q_held, q_out)]
    pairs += [(e.at[part(i)], e_held.at[part(i)], e_out.at[part(i)]) for i in range(parts)]
    ins = [pltpu.make_async_copy(src, held, come.at[i]) for i, (src, held, _) in enumerate(pairs)]
    outs = [pltpu.make_async_copy(held, dst, go.at[i]) for i, (_, held, dst) in enumerate(pairs)]
    for copy in ins:
        copy.start()
    for copy, onward in zip(ins, outs):
        copy.wait()
        onward.start()
    for copy in outs:
        copy.wait()


def shards(sizes, heads_out, grad_out, error, q_warm):
    ny, nx, nz = sizes
    tokens, m = heads_out.shape
    bk, width = grad_out.shape
    rank = q_warm.shape[1]
    nc = 2 * ny
    w = width // nc
    half = rank // 2
    eighth = half // nx
    hop = nz // 2
    y_width = 2 * w // ny
    count = nc * ny // 2
    pairs = (ny + 1) // 2
    dma = pltpu.SemaphoreType.DMA
    vmem = pltpu.VMEM
    hbm = pl.BlockSpec(memory_space=pl.ANY)
    outs = (
        jax.ShapeDtypeStruct((rank, m), F32),
        jax.ShapeDtypeStruct((1, rank, width // (ny * nx * 2)), F32),
        jax.ShapeDtypeStruct((1, m, width), BF16),
    )
    results = pl.pallas_call(
        functools.partial(kernel, sizes),
        out_shape=outs,
        in_specs=[hbm] * 4,
        out_specs=(hbm, pl.BlockSpec(memory_space=vmem), hbm),
        scratch_shapes=[
            vmem((nc, bk, w), BF16),
            vmem((2 * (hop - 1) + 1, nc, bk, w), BF16),
            vmem((tokens, m), BF16),
            vmem((nz, m, bk), BF16),
            vmem((nc, m, w), BF16),
            vmem((nc, m, w), F32),
            vmem((nc, rank, w), F32),
            vmem((nc, 2 * rank, w), BF16),
            vmem((2 * rank, tokens), F32),
            vmem((2 * rank, m), F32),
            vmem((rank, m), F32),
            vmem((2 * nx, eighth, m), F32),
            vmem((ny, eighth, m), F32),
            vmem((rank, m), F32),
            vmem((rank, m + 128), F32),
            vmem((count, rank, y_width), F32),
            vmem((count, half, y_width), F32),
            vmem((pairs, nx, ny, eighth, y_width), F32),
            vmem((pairs, ny, ny, eighth, y_width), F32),
            vmem((pairs, ny, half, y_width), F32),
            vmem((pairs, nx, half, y_width), F32),
            vmem((count, rank, y_width), F32),
            vmem((nz, 8, 128), F32),
            vmem((2, 8, 128), F32),
            vmem((nc, rank, w), F32),
            vmem((rank, bk), F32),
            vmem((rank, bk), F32),
            dma((4, nc)),
            dma((nc,)),
            dma((2, hop, nc)),
            dma((2, hop, nc)),
            dma((3, max(2 * nx, ny))),
            dma((3, max(2 * nx, ny))),
            dma((nc // 2, 4, max(nx, ny))),
            dma((nc // 2, 4, max(nx, ny))),
            dma((nc,)),
            dma((nc,)),
            dma((nz,)),
            dma((nz,)),
            dma((nx + ny + 1,)),
            dma((nx + ny + 1,)),
        ],
        compiler_params=pltpu.CompilerParams(
            collective_id=0, has_side_effects=True, vmem_limit_bytes=58 * 2**20
        ),
    )(heads_out, grad_out, error, q_warm)
    parts = 6 if m % 96 == 0 else 4
    return pl.pallas_call(
        hand_over,
        out_shape=outs,
        in_specs=[hbm] * 3,
        out_specs=(hbm,) * 3,
        scratch_shapes=[vmem(out.shape, out.dtype) for out in outs] + [dma((parts + 2,)), dma((parts + 2,))],
        compiler_params=pltpu.CompilerParams(vmem_limit_bytes=60 * 2**20),
    )(*results)


def solution(mesh, ny=4, nx=4):
    placed = (
        P("dp", "tensor"),
        P(("dp", "tensor"), None),
        P("dp", "tensor", None),
        P("tensor", None, None),
    )
    return jax.shard_map(
        functools.partial(shards, (ny, nx, mesh.shape["tensor"])),
        mesh=mesh,
        in_specs=placed,
        out_specs=(P(None, "tensor"), P("tensor", None, "dp"), P("dp", "tensor", None)),
        check_vma=False,
    )
```

```python
import functools

import jax
import jax.numpy as jnp
from jax import lax
from jax.experimental import pallas as pl
from jax.experimental.pallas import tpu as pltpu
from jax.sharding import PartitionSpec as P

MESH = pl.DeviceIdType.MESH
F32 = jnp.float32
BF16 = jnp.bfloat16


def split(value):
    high = value.astype(BF16)
    return high, (value - high.astype(F32)).astype(BF16)


def dot(a, b, a_dim, b_dim, **options):
    return lax.dot_general(a, b, (((a_dim,), (b_dim,)), ((), ())), preferred_element_type=F32, **options)


def triple(value):
    first = value.astype(BF16).astype(F32)
    rest = value - first
    second = rest.astype(BF16).astype(F32)
    return first, second, rest - second


def orthonormal(ch, rows, cols):
    place = lax.broadcasted_iota(jnp.int32, (8, 1), 0)
    tiles = range(ch.shape[1] // 128)

    def block(r, carry):
        start = pl.multiple_of(r * 8, 8)
        top = ch[pl.ds(start, 8), :]
        near = pltpu.roll(top[:, cols:], (128 - r * 8) % 128, 1)
        a = [[jnp.broadcast_to(near[i : i + 1, j : j + 1], (8, 128)) if j >= i else None for j in range(8)] for i in range(8)]
        inverse, upper = [], []
        for i in range(8):
            inverse.append(lax.rsqrt(a[i][i]))
            upper.append([a[i][j] * inverse[i] if j > i else None for j in range(8)])
            for j in range(i + 1, 8):
                for n in range(j, 8):
                    a[j][n] = a[j][n] - upper[i][j] * upper[i][n]
        done, result = [], [jnp.zeros((8, 128), F32) for _ in tiles]
        for i in range(8):
            row = [jnp.broadcast_to(top[i : i + 1, t * 128 : t * 128 + 128], (8, 128)) for t in tiles]
            for j in range(i):
                row = [row[t] - upper[j][i] * done[j][t] for t in tiles]
            row = [row[t] * inverse[i] for t in tiles]
            done.append(row)
            result = [jnp.where(place == i, row[t], result[t]) for t in tiles]
        top = jnp.concatenate(result, axis=1)
        ch[pl.ds(start, 8), :] = top
        a1, a2, a3 = triple(top[:, cols : cols + rows])
        b1, b2, b3 = triple(top)
        left = jnp.concatenate([a1, a1, a1, a2, a2, a3], axis=0).astype(BF16)
        right = jnp.concatenate([b1, b2, b3, b1, b2, b1], axis=0).astype(BF16)
        below = lax.broadcasted_iota(jnp.int32, (rows, 1), 0) >= (r + 1) * 8
        ch[...] = jnp.where(below, ch[...] - dot(left, right, 0, 0), ch[...])
        return carry

    lax.fori_loop(0, rows // 8, block, 0)


def kernel(
    sizes, heads, grad, err, q, p_out, q_out, e_out,
    own, gath, hv, at, ev, acc, qv, qs, g, pe, pt, pr, py, pf, ch,
    f, fc, xa, sa, yb, sb, ff, en, eh, qo, gs, gr,
    in_sem, out_sem, ring_send, ring_recv, p_send, p_recv, f_send, f_recv, c_send, c_recv, e_send, e_recv, q_send, q_recv,
):
    ny, nx, nz = sizes
    nc = 2 * ny
    bk, w = own.shape[1], own.shape[2]
    rank = qv.shape[1]
    half = rank // 2
    eighth = half // nx
    hop = nz // 2
    replicas = ny * nx * 2
    k, z = lax.axis_index("dp"), lax.axis_index("tensor")
    core, x, y = k % 2, (k // 2) % nx, k // (2 * nx)

    def at_dp(y_to, x_to, core_to):
        return ((y_to * nx + x_to) * 2 + core_to, z)

    other_core = at_dp(y, x, 1 - core)
    x_peer = [None] + [at_dp(y, (x + d) % nx, core) for d in range(1, nx)]
    y_peer = [None] + [at_dp((y + d) % ny, x, core) for d in range(1, ny)]
    row_len = 2 * nx
    row_at = x * 2 + core
    row_of = [(row_at + d) % row_len for d in range(row_len)]
    row_peer = [None] + [at_dp(y, row_of[d] // 2, row_of[d] % 2) for d in range(1, row_len)]
    z_peer = [None] + [(k, (z + d) % nz) for d in range(1, nz)]

    def remote(src, dst, send, recv, device):
        return pltpu.make_async_remote_copy(
            src_ref=src, dst_ref=dst, send_sem=send, recv_sem=recv, device_id=device, device_id_type=MESH
        )

    def loop(begin, end):
        def run(body):
            def step(c, carry):
                body(c)
                return carry

            lax.fori_loop(begin, end, step, 0)

        return run

    chunk_loop = loop(0, nc)
    window = min(4, nc // 2)

    def cols(c):
        return pl.ds(pl.multiple_of(c * w, w), w)

    def load_own(c):
        return pltpu.make_async_copy(grad.at[:, cols(c)], own.at[c], in_sem.at[0, c])

    def load_err(c):
        return pltpu.make_async_copy(err.at[0, :, cols(c)], ev.at[c], in_sem.at[1, c])

    def load_q(c):
        return pltpu.make_async_copy(q.at[0, :, cols(c)], qv.at[c], in_sem.at[2, c])

    load_heads = pltpu.make_async_copy(heads, hv, in_sem.at[3, 0])

    barrier = pltpu.get_barrier_semaphore()
    everyone = row_peer[1:] + y_peer[1:] + z_peer[1:]
    for device in everyone:
        pl.semaphore_signal(barrier, inc=1, device_id=device, device_id_type=MESH)

    load_heads.start()

    @chunk_loop
    def _(c):
        load_own(c).start()
        load_q(c).start()
        load_err(c).start()

    pl.semaphore_wait(barrier, len(everyone))

    far = 2 * (hop - 1)

    def slot(way, s):
        return way * (hop - 1) + s - 1

    def ring(way, s, c):
        part = pl.ds(way * (bk // 2), bk // 2)
        if s == 0:
            src = grad.at[:, cols(c)]
        else:
            src = gath.at[slot(way, s), c]
        if s == hop - 1:
            if s == 0:
                src = grad.at[part, cols(c)]
            else:
                src = gath.at[slot(way, s), c, part]
            dst = gath.at[far, c, part]
        else:
            dst = gath.at[slot(way, s + 1), c]
        return remote(src, dst, ring_send.at[way, s, c], ring_recv.at[way, s, c], z_peer[1] if way == 0 else z_peer[nz - 1])

    mine = pl.ds(pl.multiple_of(core * half, half), half)
    theirs = pl.ds(pl.multiple_of((1 - core) * half, half), half)

    per_chunk = nx // 2
    q_width = 2 * w // nx
    q_piece = pl.ds(pl.multiple_of((y * nx + x) * q_width, q_width), q_width)
    q_place = (2 * y + x // per_chunk, mine, pl.ds(pl.multiple_of((x % per_chunk) * q_width, q_width), q_width))
    opposite = z_peer[hop]

    def q_spread(place, first, peers):
        return [
            remote(qo.at[place], qo.at[place], q_send.at[first + d], q_recv.at[first + d], peers[d])
            for d in range(1, len(peers))
        ]

    q_over_z = remote(q.at[0, mine, q_piece], qo.at[q_place], q_send.at[0], q_recv.at[0], opposite)
    q_over_x = q_spread(q_place, 0, x_peer)
    q_over_y = q_spread((pl.ds(2 * y, 2), mine), nx - 1, y_peer)
    q_over_core = q_spread((pl.ds(0, nc), mine), nx + ny - 2, [None, other_core])
    g_over_z = remote(gs, gr, q_send.at[nx + ny], q_recv.at[nx + ny], opposite)

    q_over_z.start()

    @loop(0, window)
    def _(c):
        ring(0, 0, c).start()
        ring(1, 0, c).start()

    load_heads.wait()

    def flip(i, carry):
        at[i] = hv[pl.ds(pl.multiple_of(i * bk, bk), bk), :].astype(F32).T.astype(BF16)
        return carry

    lax.fori_loop(0, nz, flip, 0)
    g[...] = jnp.zeros_like(g)
    pe[...] = jnp.zeros_like(pe)

    def use(block, c, which):
        acc[c] += dot(at[which], block, 1, 0)

    def use_both(block, c, which):
        use(block, c, which)
        place = pl.ds(pl.multiple_of(which * bk, bk), bk)
        g[:, place] += dot(qs[c], block, 1, 1)

    def own_chunk(c):
        load_q(c).wait()
        high, low = split(qv[c])
        qs[c, 0:rank, :] = high
        qs[c, rank:, :] = low
        load_err(c).wait()
        acc[c] = ev[c].astype(F32)
        pe[...] += dot(qs[c], ev[c], 1, 1)
        load_own(c).wait()
        use_both(own[c], c, z)

    @loop(0, nc - window)
    def _(c):
        own_chunk(c)
        for way in range(2):
            ring(way, 0, c).wait_send()
            ring(way, 0, c + window).start()

    loop(nc - window, nc)(own_chunk)

    def q_step_x():
        q_over_z.wait()
        for copy in q_over_x:
            copy.start()

    def q_step_y():
        for copy in q_over_x:
            copy.wait()
        for copy in q_over_y:
            copy.start()

    def q_step_core():
        for copy in q_over_y:
            copy.wait()
        for copy in q_over_core:
            copy.start()
        for copy in q_over_core:
            copy.wait()

        def term(c, total):
            high, low = split(qo[c])
            return total + dot(jnp.concatenate([high, low], axis=0), own[c], 1, 1)

        total = lax.fori_loop(0, nc, term, jnp.zeros((2 * rank, bk), F32))
        gs[...] = total[0:rank] + total[rank:]
        g_over_z.start()

    q_step_x()
    steps = [q_step_y, q_step_core]

    def ring_chunk(s, before, begin=0, end=0):
        def run(c):
            for way in range(2):
                ring(way, s - 1, c).wait_recv()
                if before is not None:
                    ring(way, *before(c)).wait_send()
                    ring(way, s, c).start()
            for other in range(begin, end):
                ring(0, s, other).start()
                ring(1, s, other).start()
            use_both(gath[slot(0, s), c], c, (z - s + nz) % nz)
            use_both(gath[slot(1, s), c], c, (z + s) % nz)

        return run

    for s in range(1, hop):
        if s < hop - 1:
            loop(0, window)(ring_chunk(s, lambda c: (s - 1, nc - window + c)))
            loop(window, nc)(ring_chunk(s, lambda c: (s, c - window)))
        else:
            late = min(3, nc - 1)
            loop(0, nc - late)(ring_chunk(s, None))
            for i in range(late):
                ring_chunk(s, None, i * nc // 4, (i + 1) * nc // 4 if i < late - 1 else nc)(nc - late + i)
        if steps:
            steps.pop(0)()
    for step in steps:
        step()
    g_over_z.wait()
    g[0:rank, pl.ds(pl.multiple_of(((z + hop) % nz) * bk, bk), bk)] = gr[...]

    def rows_of(core_at, x_at):
        return pl.ds(pl.multiple_of(core_at * half + x_at * eighth, eighth), eighth)

    rows = rows_of(core, x)

    def run_all(copies):
        for copy in copies:
            copy.start()
        for copy in copies:
            copy.wait()

    def total_of(ref, count):
        return functools.reduce(lambda a, b: a + b, [ref[i] for i in range(count)])

    total = g[0:rank, :] + g[rank:, :]
    high, low = split(total)
    terms = dot(jnp.concatenate([high, low], axis=0), hv[...], 1, 0) + pe[...]
    pt[...] = terms[0:rank, :] + terms[rank:, :]
    pr[row_at] = pt[rows, :]
    run_all([
        remote(pt.at[rows_of(row_of[d] % 2, row_of[d] // 2)], pr.at[row_at], p_send.at[0, d], p_recv.at[0, d], row_peer[d])
        for d in range(1, row_len)
    ])
    py[y] = total_of(pr, row_len)
    run_all([remote(py.at[y], py.at[y], p_send.at[1, d], p_recv.at[1, d], y_peer[d]) for d in range(1, ny)])
    pf[rows, :] = total_of(py, ny)
    run_all([remote(pf.at[rows], pf.at[rows], p_send.at[2, d], p_recv.at[2, d], row_peer[d]) for d in range(1, row_len)])

    m = pf.shape[1]
    ch[:, 0:m] = pf[...]
    ch[:, m:] = jnp.zeros((rank, 128), F32)
    ch[:, m : m + rank] = dot(pf[...], pf[...], 1, 1, precision=lax.Precision.HIGHEST)
    orthonormal(ch, rank, m)
    basis = ch[:, 0:m]
    basis_out = pltpu.make_async_copy(ch.at[:, pl.ds(0, m)], p_out, in_sem.at[3, 1])
    basis_out.start()
    b_high, b_low = split(basis)
    b_both = jnp.concatenate([b_high, b_low], axis=0)

    per = ny // 2
    y_width = w // per
    groups = nc // 2

    def in_chunk(c):
        return pl.ds(c * per, per)

    def core_copy(c):
        return remote(f.at[in_chunk(c), theirs], fc.at[in_chunk(c)], c_send.at[c], c_recv.at[c], other_core)

    def factor_chunk(c):
        ring(0, hop - 1, c).wait_recv()
        ring(1, hop - 1, c).wait_recv()
        use(gath[far, c], c, (z + hop) % nz)
        high, low = split(acc[c])
        both = dot(b_both, high, 1, 0)
        both = (both[0:rank] + both[rank:] + dot(b_high, low, 1, 0)) * (1.0 / replicas)
        for i in range(per):
            f[c * per + i] = both[:, i * y_width : (i + 1) * y_width]
        core_copy(c).start()

    def spread(place, i, stage, peers):
        return [
            remote(ff.at[place], ff.at[place], f_send.at[i, stage, d], f_recv.at[i, stage, d], peers[d])
            for d in range(1, len(peers))
        ]

    def squares(i, carry):
        value = ff[i, mine, :]
        return carry + jnp.sum(value * value, axis=(0, 1), keepdims=True)

    class Group:
        def __init__(self, i):
            self.i = i
            self.base = i * ny
            self.whole = pl.ds(i * ny, ny)

        def first(self):
            i = self.i

            @loop(2 * i, 2 * i + 2)
            def _(c):
                core_copy(c).wait()

            f[self.whole, mine, :] += fc[self.whole]
            if i % 2 == 0:
                xa[i // 2, x] = f[self.whole, rows, :]
                self.copies = [
                    remote(f.at[self.whole, rows_of(core, (x + d) % nx)], xa.at[i // 2, x], f_send.at[i, 0, d], f_recv.at[i, 0, d], x_peer[d])
                    for d in range(1, nx)
                ]
            else:
                yb[i // 2, y] = f[self.base + y, mine, :]
                self.copies = [
                    remote(f.at[self.base + (y + d) % ny, mine], yb.at[i // 2, y], f_send.at[i, 0, d], f_recv.at[i, 0, d], y_peer[d])
                    for d in range(1, ny)
                ]
            self.start()

        def second(self):
            self.wait()
            i = self.i
            if i % 2 == 0:
                sa[i // 2, y] = total_of(xa.at[i // 2], nx)
                mine_now, peers = sa.at[i // 2, y], y_peer
            else:
                sb[i // 2, x] = total_of(yb.at[i // 2], ny)
                mine_now, peers = sb.at[i // 2, x], x_peer
            self.copies = [
                remote(mine_now, mine_now, f_send.at[i, 1, d], f_recv.at[i, 1, d], peers[d]) for d in range(1, len(peers))
            ]
            self.start()

        def third(self):
            self.wait()
            i = self.i
            if i % 2 == 0:
                ff[self.whole, rows, :] = total_of(sa.at[i // 2], ny)
                self.copies = spread((self.whole, rows), i, 2, x_peer)
            else:
                ff[self.base + y, mine, :] = total_of(sb.at[i // 2], nx)
                self.copies = spread((self.base + y, mine), i, 2, y_peer)
            self.start()

        def fourth(self):
            self.wait()
            self.energy = lax.fori_loop(self.base, self.base + ny, squares, jnp.zeros((1, 1), F32))
            self.copies = spread((self.whole, mine), self.i, 3, [None, other_core])
            self.start()

        def start(self):
            for copy in self.copies:
                copy.start()

        def wait(self):
            for copy in self.copies:
                copy.wait()

    every = [Group(i) for i in range(groups)]
    for group in every:
        loop(2 * group.i, 2 * group.i + 2)(factor_chunk)
        if group.i > 0:
            every[group.i - 1].first()
    every[-1].first()
    for group in every:
        group.second()
    for group in every:
        group.third()

    b_wide = jnp.concatenate([b_high, b_high, b_low], axis=0).astype(F32).T.astype(BF16)

    def store(c):
        return pltpu.make_async_copy(ev.at[c], e_out.at[0, :, cols(c)], out_sem.at[c])

    def last_chunk(c):
        high, low = split(jnp.concatenate([ff[c * per + i] for i in range(per)], axis=1))
        approx = dot(b_wide, jnp.concatenate([high, low, high], axis=0), 1, 0)
        ev[c] = (acc[c] - approx).astype(BF16)
        store(c).start()

    def finish(group):
        group.wait()
        loop(2 * group.i, 2 * group.i + 2)(last_chunk)

    for group in every[:-1]:
        group.fourth()
        if group.i > 0:
            finish(every[group.i - 1])
    every[-1].fourth()
    energy = functools.reduce(lambda a, b: a + b, [group.energy for group in every])
    en[z] = jnp.broadcast_to(energy, (8, 128))
    energies = [remote(en.at[z], en.at[z], e_send.at[d], e_recv.at[d], z_peer[d]) for d in range(1, nz)]
    for copy in energies:
        copy.start()
    for group in every[max(groups - 2, 0) :]:
        finish(group)
    for copy in energies:
        copy.wait()
    eh[core] = total_of(en, nz)
    run_all([remote(eh.at[core], eh.at[core], e_send.at[0], e_recv.at[0], other_core)])
    entire = (eh[0] + eh[1])[0:1, 0:1]
    scale = lax.rsqrt(entire * (1.0 / (m * nz * w * nc)) + 1e-06)
    width = q_out.shape[2]
    ahead = y_width // width
    piece = ff[k // ahead]
    piece = pltpu.roll(piece, (y_width - (k % ahead) * width) % y_width, 1)
    q_out[0] = piece[:, 0:width] * scale

    @loop(nc - window, nc)
    def _(c):
        ring(0, hop - 2, c).wait_send()
        ring(1, hop - 2, c).wait_send()

    @chunk_loop
    def _(c):
        ring(0, hop - 1, c).wait_send()
        ring(1, hop - 1, c).wait_send()

    @chunk_loop
    def _(c):
        store(c).wait()

    basis_out.wait()


def hand_over(p, q, e, p_out, q_out, e_out, p_held, q_held, e_held, come, go):
    parts = go.shape[0] - 2
    rows = e_held.shape[1] // parts

    def part(i):
        return (0, pl.ds(i * rows, rows))

    pairs = [(p, p_held, p_out), (q, q_held, q_out)]
    pairs += [(e.at[part(i)], e_held.at[part(i)], e_out.at[part(i)]) for i in range(parts)]
    ins = [pltpu.make_async_copy(src, held, come.at[i]) for i, (src, held, _) in enumerate(pairs)]
    outs = [pltpu.make_async_copy(held, dst, go.at[i]) for i, (_, held, dst) in enumerate(pairs)]
    for copy in ins:
        copy.start()
    for copy, onward in zip(ins, outs):
        copy.wait()
        onward.start()
    for copy in outs:
        copy.wait()


def shards(sizes, heads_out, grad_out, error, q_warm):
    ny, nx, nz = sizes
    tokens, m = heads_out.shape
    bk, width = grad_out.shape
    rank = q_warm.shape[1]
    nc = 2 * ny
    w = width // nc
    half = rank // 2
    eighth = half // nx
    hop = nz // 2
    y_width = 2 * w // ny
    count = nc * ny // 2
    pairs = (ny + 1) // 2
    dma = pltpu.SemaphoreType.DMA
    vmem = pltpu.VMEM
    hbm = pl.BlockSpec(memory_space=pl.ANY)
    outs = (
        jax.ShapeDtypeStruct((rank, m), F32),
        jax.ShapeDtypeStruct((1, rank, width // (ny * nx * 2)), F32),
        jax.ShapeDtypeStruct((1, m, width), BF16),
    )
    results = pl.pallas_call(
        functools.partial(kernel, sizes),
        out_shape=outs,
        in_specs=[hbm] * 4,
        out_specs=(hbm, pl.BlockSpec(memory_space=vmem), hbm),
        scratch_shapes=[
            vmem((nc, bk, w), BF16),
            vmem((2 * (hop - 1) + 1, nc, bk, w), BF16),
            vmem((tokens, m), BF16),
            vmem((nz, m, bk), BF16),
            vmem((nc, m, w), BF16),
            vmem((nc, m, w), F32),
            vmem((nc, rank, w), F32),
            vmem((nc, 2 * rank, w), BF16),
            vmem((2 * rank, tokens), F32),
            vmem((2 * rank, m), F32),
            vmem((rank, m), F32),
            vmem((2 * nx, eighth, m), F32),
            vmem((ny, eighth, m), F32),
            vmem((rank, m), F32),
            vmem((rank, m + 128), F32),
            vmem((count, rank, y_width), F32),
            vmem((count, half, y_width), F32),
            vmem((pairs, nx, ny, eighth, y_width), F32),
            vmem((pairs, ny, ny, eighth, y_width), F32),
            vmem((pairs, ny, half, y_width), F32),
            vmem((pairs, nx, half, y_width), F32),
            vmem((count, rank, y_width), F32),
            vmem((nz, 8, 128), F32),
            vmem((2, 8, 128), F32),
            vmem((nc, rank, w), F32),
            vmem((rank, bk), F32),
            vmem((rank, bk), F32),
            dma((4, nc)),
            dma((nc,)),
            dma((2, hop, nc)),
            dma((2, hop, nc)),
            dma((3, max(2 * nx, ny))),
            dma((3, max(2 * nx, ny))),
            dma((nc // 2, 4, max(nx, ny))),
            dma((nc // 2, 4, max(nx, ny))),
            dma((nc,)),
            dma((nc,)),
            dma((nz,)),
            dma((nz,)),
            dma((nx + ny + 1,)),
            dma((nx + ny + 1,)),
        ],
        compiler_params=pltpu.CompilerParams(
            collective_id=0, has_side_effects=True, vmem_limit_bytes=58 * 2**20
        ),
    )(heads_out, grad_out, error, q_warm)
    parts = 6 if m % 96 == 0 else 4
    return pl.pallas_call(
        hand_over,
        out_shape=outs,
        in_specs=[hbm] * 3,
        out_specs=(hbm,) * 3,
        scratch_shapes=[vmem(out.shape, out.dtype) for out in outs] + [dma((parts + 2,)), dma((parts + 2,))],
        compiler_params=pltpu.CompilerParams(vmem_limit_bytes=60 * 2**20),
    )(*results)


def solution(mesh, ny=4, nx=4):
    placed = (
        P("dp", "tensor"),
        P(("dp", "tensor"), None),
        P("dp", "tensor", None),
        P("tensor", None, None),
    )
    return jax.shard_map(
        functools.partial(shards, (ny, nx, mesh.shape["tensor"])),
        mesh=mesh,
        in_specs=placed,
        out_specs=(P(None, "tensor"), P("tensor", None, "dp"), P("dp", "tensor", None)),
        check_vma=False,
    )
```

```python
import functools

import jax
import jax.numpy as jnp
from jax import lax
from jax.experimental import pallas as pl
from jax.experimental.pallas import tpu as pltpu
from jax.sharding import PartitionSpec as P

MESH = pl.DeviceIdType.MESH
F32 = jnp.float32
BF16 = jnp.bfloat16


def split(value):
    high = value.astype(BF16)
    return high, (value - high.astype(F32)).astype(BF16)


def dot(a, b, a_dim, b_dim, **options):
    return lax.dot_general(a, b, (((a_dim,), (b_dim,)), ((), ())), preferred_element_type=F32, **options)


def triple(value):
    first = value.astype(BF16).astype(F32)
    rest = value - first
    second = rest.astype(BF16).astype(F32)
    return first, second, rest - second


def orthonormal(ch, rows, cols):
    place = lax.broadcasted_iota(jnp.int32, (8, 1), 0)
    tiles = range(ch.shape[1] // 128)

    def block(r, carry):
        start = pl.multiple_of(r * 8, 8)
        top = ch[pl.ds(start, 8), :]
        near = pltpu.roll(top[:, cols:], (128 - r * 8) % 128, 1)
        a = [[jnp.broadcast_to(near[i : i + 1, j : j + 1], (8, 128)) if j >= i else None for j in range(8)] for i in range(8)]
        inverse, upper = [], []
        for i in range(8):
            inverse.append(lax.rsqrt(a[i][i]))
            upper.append([a[i][j] * inverse[i] if j > i else None for j in range(8)])
            for j in range(i + 1, 8):
                for n in range(j, 8):
                    a[j][n] = a[j][n] - upper[i][j] * upper[i][n]
        done, result = [], [jnp.zeros((8, 128), F32) for _ in tiles]
        for i in range(8):
            row = [jnp.broadcast_to(top[i : i + 1, t * 128 : t * 128 + 128], (8, 128)) for t in tiles]
            for j in range(i):
                row = [row[t] - upper[j][i] * done[j][t] for t in tiles]
            row = [row[t] * inverse[i] for t in tiles]
            done.append(row)
            result = [jnp.where(place == i, row[t], result[t]) for t in tiles]
        top = jnp.concatenate(result, axis=1)
        ch[pl.ds(start, 8), :] = top
        a1, a2, a3 = triple(top[:, cols : cols + rows])
        b1, b2, b3 = triple(top)
        left = jnp.concatenate([a1, a1, a1, a2, a2, a3], axis=0).astype(BF16)
        right = jnp.concatenate([b1, b2, b3, b1, b2, b1], axis=0).astype(BF16)
        below = lax.broadcasted_iota(jnp.int32, (rows, 1), 0) >= (r + 1) * 8
        ch[...] = jnp.where(below, ch[...] - dot(left, right, 0, 0), ch[...])
        return carry

    lax.fori_loop(0, rows // 8, block, 0)


def kernel(
    sizes, heads, grad, err, q, p_out, q_out, e_out,
    own, gath, hv, at, ev, acc, qv, qs, g, pe, pt, pr, py, pf, ch,
    f, fc, xa, sa, yb, sb, ff, en, eh, qo, gs, gr,
    in_sem, out_sem, ring_send, ring_recv, p_send, p_recv, f_send, f_recv, c_send, c_recv, e_send, e_recv, q_send, q_recv,
):
    ny, nx, nz = sizes
    nc = 2 * ny
    bk, w = own.shape[1], own.shape[2]
    rank = qv.shape[1]
    half = rank // 2
    eighth = half // nx
    hop = nz // 2
    replicas = ny * nx * 2
    k, z = lax.axis_index("dp"), lax.axis_index("tensor")
    core, x, y = k % 2, (k // 2) % nx, k // (2 * nx)

    def at_dp(y_to, x_to, core_to):
        return ((y_to * nx + x_to) * 2 + core_to, z)

    other_core = at_dp(y, x, 1 - core)
    x_peer = [None] + [at_dp(y, (x + d) % nx, core) for d in range(1, nx)]
    y_peer = [None] + [at_dp((y + d) % ny, x, core) for d in range(1, ny)]
    row_len = 2 * nx
    row_at = x * 2 + core
    row_of = [(row_at + d) % row_len for d in range(row_len)]
    row_peer = [None] + [at_dp(y, row_of[d] // 2, row_of[d] % 2) for d in range(1, row_len)]
    z_peer = [None] + [(k, (z + d) % nz) for d in range(1, nz)]

    def remote(src, dst, send, recv, device):
        return pltpu.make_async_remote_copy(
            src_ref=src, dst_ref=dst, send_sem=send, recv_sem=recv, device_id=device, device_id_type=MESH
        )

    def loop(begin, end, unroll=1):
        def run(body):
            def step(c, carry):
                body(c)
                return carry

            lax.fori_loop(begin, end, step, 0, unroll=unroll)

        return run

    chunk_loop = loop(0, nc)
    window = min(4, nc // 2)

    def cols(c):
        return pl.ds(pl.multiple_of(c * w, w), w)

    def load_own(c):
        return pltpu.make_async_copy(grad.at[:, cols(c)], own.at[c], in_sem.at[0, c])

    def load_err(c):
        return pltpu.make_async_copy(err.at[0, :, cols(c)], ev.at[c], in_sem.at[1, c])

    def load_q(c):
        return pltpu.make_async_copy(q.at[0, :, cols(c)], qv.at[c], in_sem.at[2, c])

    load_heads = pltpu.make_async_copy(heads, hv, in_sem.at[3, 0])

    barrier = pltpu.get_barrier_semaphore()
    everyone = row_peer[1:] + y_peer[1:] + z_peer[1:]
    for device in everyone:
        pl.semaphore_signal(barrier, inc=1, device_id=device, device_id_type=MESH)

    load_heads.start()

    @chunk_loop
    def _(c):
        load_own(c).start()
        load_q(c).start()
        load_err(c).start()

    pl.semaphore_wait(barrier, len(everyone))

    far = 2 * (hop - 1)

    def slot(way, s):
        return way * (hop - 1) + s - 1

    def ring(way, s, c):
        part = pl.ds(way * (bk // 2), bk // 2)
        if s == 0:
            src = grad.at[:, cols(c)]
        else:
            src = gath.at[slot(way, s), c]
        if s == hop - 1:
            if s == 0:
                src = grad.at[part, cols(c)]
            else:
                src = gath.at[slot(way, s), c, part]
            dst = gath.at[far, c, part]
        else:
            dst = gath.at[slot(way, s + 1), c]
        return remote(src, dst, ring_send.at[way, s, c], ring_recv.at[way, s, c], z_peer[1] if way == 0 else z_peer[nz - 1])

    mine = pl.ds(pl.multiple_of(core * half, half), half)
    theirs = pl.ds(pl.multiple_of((1 - core) * half, half), half)

    per_chunk = nx // 2
    q_width = 2 * w // nx
    q_piece = pl.ds(pl.multiple_of((y * nx + x) * q_width, q_width), q_width)
    q_place = (2 * y + x // per_chunk, mine, pl.ds(pl.multiple_of((x % per_chunk) * q_width, q_width), q_width))
    opposite = z_peer[hop]

    def q_spread(place, first, peers):
        return [
            remote(qo.at[place], qo.at[place], q_send.at[first + d], q_recv.at[first + d], peers[d])
            for d in range(1, len(peers))
        ]

    q_over_z = remote(q.at[0, mine, q_piece], qo.at[q_place], q_send.at[0], q_recv.at[0], opposite)
    q_over_x = q_spread(q_place, 0, x_peer)
    q_over_y = q_spread((pl.ds(2 * y, 2), mine), nx - 1, y_peer)
    q_over_core = q_spread((pl.ds(0, nc), mine), nx + ny - 2, [None, other_core])
    g_over_z = remote(gs, gr, q_send.at[nx + ny], q_recv.at[nx + ny], opposite)

    q_over_z.start()

    @loop(0, window)
    def _(c):
        ring(0, 0, c).start()
        ring(1, 0, c).start()

    load_heads.wait()

    def flip(i, carry):
        at[i] = hv[pl.ds(pl.multiple_of(i * bk, bk), bk), :].astype(F32).T.astype(BF16)
        return carry

    lax.fori_loop(0, nz, flip, 0)
    g[...] = jnp.zeros_like(g)
    pe[...] = jnp.zeros_like(pe)

    def use(block, c, which):
        acc[c] += dot(at[which], block, 1, 0)

    def use_both(block, c, which):
        use(block, c, which)
        place = pl.ds(pl.multiple_of(which * bk, bk), bk)
        g[:, place] += dot(qs[c], block, 1, 1)

    def own_chunk(c):
        load_q(c).wait()
        high, low = split(qv[c])
        qs[c, 0:rank, :] = high
        qs[c, rank:, :] = low
        load_err(c).wait()
        acc[c] = ev[c].astype(F32)
        pe[...] += dot(qs[c], ev[c], 1, 1)
        load_own(c).wait()
        use_both(own[c], c, z)

    @loop(0, nc - window)
    def _(c):
        own_chunk(c)
        for way in range(2):
            ring(way, 0, c).wait_send()
            ring(way, 0, c + window).start()

    loop(nc - window, nc)(own_chunk)

    def q_step_x():
        q_over_z.wait()
        for copy in q_over_x:
            copy.start()

    def q_step_y():
        for copy in q_over_x:
            copy.wait()
        for copy in q_over_y:
            copy.start()

    def q_step_core():
        for copy in q_over_y:
            copy.wait()
        for copy in q_over_core:
            copy.start()
        for copy in q_over_core:
            copy.wait()

        def term(c, total):
            high, low = split(qo[c])
            return total + dot(jnp.concatenate([high, low], axis=0), own[c], 1, 1)

        total = lax.fori_loop(0, nc, term, jnp.zeros((2 * rank, bk), F32))
        gs[...] = total[0:rank] + total[rank:]
        g_over_z.start()

    q_step_x()
    steps = [q_step_y, q_step_core]

    def ring_chunk(s, before, begin=0, end=0):
        def run(c):
            for way in range(2):
                ring(way, s - 1, c).wait_recv()
                if before is not None:
                    ring(way, *before(c)).wait_send()
                    ring(way, s, c).start()
            for other in range(begin, end):
                ring(0, s, other).start()
                ring(1, s, other).start()
            use_both(gath[slot(0, s), c], c, (z - s + nz) % nz)
            use_both(gath[slot(1, s), c], c, (z + s) % nz)

        return run

    for s in range(1, hop):
        if s < hop - 1:
            loop(0, window)(ring_chunk(s, lambda c: (s - 1, nc - window + c)))
            loop(window, nc)(ring_chunk(s, lambda c: (s, c - window)))
        else:
            late = min(3, nc - 1)
            loop(0, nc - late)(ring_chunk(s, None))
            for i in range(late):
                ring_chunk(s, None, i * nc // 4, (i + 1) * nc // 4 if i < late - 1 else nc)(nc - late + i)
        if steps:
            steps.pop(0)()
    for step in steps:
        step()
    g_over_z.wait()
    g[0:rank, pl.ds(pl.multiple_of(((z + hop) % nz) * bk, bk), bk)] = gr[...]

    def rows_of(core_at, x_at):
        return pl.ds(pl.multiple_of(core_at * half + x_at * eighth, eighth), eighth)

    rows = rows_of(core, x)

    def far_chunk(c):
        ring(0, hop - 1, c).wait_recv()
        ring(1, hop - 1, c).wait_recv()
        use(gath[far, c], c, (z + hop) % nz)

    def run_all(copies, meanwhile=None):
        for copy in copies:
            copy.start()
        if meanwhile is not None:
            meanwhile(far_chunk)
        for copy in copies:
            copy.wait()

    def total_of(ref, count):
        return functools.reduce(lambda a, b: a + b, [ref[i] for i in range(count)])

    total = g[0:rank, :] + g[rank:, :]
    high, low = split(total)
    terms = dot(jnp.concatenate([high, low], axis=0), hv[...], 1, 0) + pe[...]
    pt[...] = terms[0:rank, :] + terms[rank:, :]
    pr[row_at] = pt[rows, :]
    run_all([
        remote(pt.at[rows_of(row_of[d] % 2, row_of[d] // 2)], pr.at[row_at], p_send.at[0, d], p_recv.at[0, d], row_peer[d])
        for d in range(1, row_len)
    ])
    py[y] = total_of(pr, row_len)
    run_all([remote(py.at[y], py.at[y], p_send.at[1, d], p_recv.at[1, d], y_peer[d]) for d in range(1, ny)], loop(0, nc // 4))
    pf[rows, :] = total_of(py, ny)
    run_all([remote(pf.at[rows], pf.at[rows], p_send.at[2, d], p_recv.at[2, d], row_peer[d]) for d in range(1, row_len)], loop(nc // 4, nc // 2))

    m = pf.shape[1]
    ch[:, 0:m] = pf[...]
    ch[:, m:] = jnp.zeros((rank, 128), F32)
    ch[:, m : m + rank] = dot(pf[...], pf[...], 1, 1, precision=lax.Precision.HIGHEST)
    orthonormal(ch, rank, m)
    basis = ch[:, 0:m]
    basis_out = pltpu.make_async_copy(ch.at[:, pl.ds(0, m)], p_out, in_sem.at[3, 1])
    basis_out.start()
    b_high, b_low = split(basis)
    b_both = jnp.concatenate([b_high, b_low], axis=0)

    per = ny // 2
    y_width = w // per
    groups = nc // 2

    def in_chunk(c):
        return pl.ds(c * per, per)

    def core_copy(c):
        return remote(f.at[in_chunk(c), theirs], fc.at[in_chunk(c)], c_send.at[c], c_recv.at[c], other_core)

    def factor_chunk(c, early):
        if not early:
            far_chunk(c)
        high, low = split(acc[c])
        both = dot(b_both, high, 1, 0)
        both = (both[0:rank] + both[rank:] + dot(b_high, low, 1, 0)) * (1.0 / replicas)
        for i in range(per):
            f[c * per + i] = both[:, i * y_width : (i + 1) * y_width]
        core_copy(c).start()

    def spread(place, i, stage, peers):
        return [
            remote(ff.at[place], ff.at[place], f_send.at[i, stage, d], f_recv.at[i, stage, d], peers[d])
            for d in range(1, len(peers))
        ]

    def squares(i, carry):
        value = ff[i, mine, :]
        return carry + jnp.sum(value * value, axis=(0, 1), keepdims=True)

    class Group:
        def __init__(self, i):
            self.i = i
            self.base = i * ny
            self.whole = pl.ds(i * ny, ny)

        def first(self):
            i = self.i

            @loop(2 * i, 2 * i + 2)
            def _(c):
                core_copy(c).wait()

            f[self.whole, mine, :] += fc[self.whole]
            if i % 2 == 0:
                xa[i // 2, x] = f[self.whole, rows, :]
                self.copies = [
                    remote(f.at[self.whole, rows_of(core, (x + d) % nx)], xa.at[i // 2, x], f_send.at[i, 0, d], f_recv.at[i, 0, d], x_peer[d])
                    for d in range(1, nx)
                ]
            else:
                yb[i // 2, y] = f[self.base + y, mine, :]
                self.copies = [
                    remote(f.at[self.base + (y + d) % ny, mine], yb.at[i // 2, y], f_send.at[i, 0, d], f_recv.at[i, 0, d], y_peer[d])
                    for d in range(1, ny)
                ]
            self.start()

        def second(self):
            self.wait()
            i = self.i
            if i % 2 == 0:
                sa[i // 2, y] = total_of(xa.at[i // 2], nx)
                mine_now, peers = sa.at[i // 2, y], y_peer
            else:
                sb[i // 2, x] = total_of(yb.at[i // 2], ny)
                mine_now, peers = sb.at[i // 2, x], x_peer
            self.copies = [
                remote(mine_now, mine_now, f_send.at[i, 1, d], f_recv.at[i, 1, d], peers[d]) for d in range(1, len(peers))
            ]
            self.start()

        def third(self):
            self.wait()
            i = self.i
            if i % 2 == 0:
                ff[self.whole, rows, :] = total_of(sa.at[i // 2], ny)
                self.copies = spread((self.whole, rows), i, 2, x_peer)
            else:
                ff[self.base + y, mine, :] = total_of(sb.at[i // 2], nx)
                self.copies = spread((self.base + y, mine), i, 2, y_peer)
            self.start()

        def fourth(self):
            self.wait()
            self.energy = lax.fori_loop(self.base, self.base + ny, squares, jnp.zeros((1, 1), F32))
            self.copies = spread((self.whole, mine), self.i, 3, [None, other_core])
            self.start()

        def start(self):
            for copy in self.copies:
                copy.start()

        def wait(self):
            for copy in self.copies:
                copy.wait()

    every = [Group(i) for i in range(groups)]
    for group in every:
        loop(2 * group.i, 2 * group.i + 2, 2)(functools.partial(factor_chunk, early=group.i < groups // 2))
        if group.i > 0:
            every[group.i - 1].first()
    every[-1].first()
    for group in every:
        group.second()
    for group in every:
        group.third()

    b_wide = jnp.concatenate([b_high, b_high, b_low], axis=0).astype(F32).T.astype(BF16)

    def store(c):
        return pltpu.make_async_copy(ev.at[c], e_out.at[0, :, cols(c)], out_sem.at[c])

    def last_chunk(c):
        high, low = split(jnp.concatenate([ff[c * per + i] for i in range(per)], axis=1))
        approx = dot(b_wide, jnp.concatenate([high, low, high], axis=0), 1, 0)
        ev[c] = (acc[c] - approx).astype(BF16)
        store(c).start()

    def finish(group):
        group.wait()
        loop(2 * group.i, 2 * group.i + 2, 2)(last_chunk)

    for group in every[:-1]:
        group.fourth()
        if group.i > 0:
            finish(every[group.i - 1])
    every[-1].fourth()
    energy = functools.reduce(lambda a, b: a + b, [group.energy for group in every])
    en[z] = jnp.broadcast_to(energy, (8, 128))
    energies = [remote(en.at[z], en.at[z], e_send.at[d], e_recv.at[d], z_peer[d]) for d in range(1, nz)]
    for copy in energies:
        copy.start()
    for group in every[max(groups - 2, 0) :]:
        finish(group)
    for copy in energies:
        copy.wait()
    eh[core] = total_of(en, nz)
    run_all([remote(eh.at[core], eh.at[core], e_send.at[0], e_recv.at[0], other_core)])
    entire = (eh[0] + eh[1])[0:1, 0:1]
    scale = lax.rsqrt(entire * (1.0 / (m * nz * w * nc)) + 1e-06)
    width = q_out.shape[2]
    ahead = y_width // width
    piece = ff[k // ahead]
    piece = pltpu.roll(piece, (y_width - (k % ahead) * width) % y_width, 1)
    q_out[0] = piece[:, 0:width] * scale

    @loop(nc - window, nc)
    def _(c):
        ring(0, hop - 2, c).wait_send()
        ring(1, hop - 2, c).wait_send()

    @chunk_loop
    def _(c):
        ring(0, hop - 1, c).wait_send()
        ring(1, hop - 1, c).wait_send()

    @chunk_loop
    def _(c):
        store(c).wait()

    basis_out.wait()


def hand_over(p, q, e, p_out, q_out, e_out, p_held, q_held, e_held, come, go):
    parts = go.shape[0] - 2
    rows = e_held.shape[1] // parts

    def part(i):
        return (0, pl.ds(i * rows, rows))

    pairs = [(p, p_held, p_out), (q, q_held, q_out)]
    pairs += [(e.at[part(i)], e_held.at[part(i)], e_out.at[part(i)]) for i in range(parts)]
    ins = [pltpu.make_async_copy(src, held, come.at[i]) for i, (src, held, _) in enumerate(pairs)]
    outs = [pltpu.make_async_copy(held, dst, go.at[i]) for i, (_, held, dst) in enumerate(pairs)]
    for copy in ins:
        copy.start()
    for copy, onward in zip(ins, outs):
        copy.wait()
        onward.start()
    for copy in outs:
        copy.wait()


def shards(sizes, heads_out, grad_out, error, q_warm):
    ny, nx, nz = sizes
    tokens, m = heads_out.shape
    bk, width = grad_out.shape
    rank = q_warm.shape[1]
    nc = 2 * ny
    w = width // nc
    half = rank // 2
    eighth = half // nx
    hop = nz // 2
    y_width = 2 * w // ny
    count = nc * ny // 2
    pairs = (ny + 1) // 2
    dma = pltpu.SemaphoreType.DMA
    vmem = pltpu.VMEM
    hbm = pl.BlockSpec(memory_space=pl.ANY)
    outs = (
        jax.ShapeDtypeStruct((rank, m), F32),
        jax.ShapeDtypeStruct((1, rank, width // (ny * nx * 2)), F32),
        jax.ShapeDtypeStruct((1, m, width), BF16),
    )
    results = pl.pallas_call(
        functools.partial(kernel, sizes),
        out_shape=outs,
        in_specs=[hbm] * 4,
        out_specs=(hbm, pl.BlockSpec(memory_space=vmem), hbm),
        scratch_shapes=[
            vmem((nc, bk, w), BF16),
            vmem((2 * (hop - 1) + 1, nc, bk, w), BF16),
            vmem((tokens, m), BF16),
            vmem((nz, m, bk), BF16),
            vmem((nc, m, w), BF16),
            vmem((nc, m, w), F32),
            vmem((nc, rank, w), F32),
            vmem((nc, 2 * rank, w), BF16),
            vmem((2 * rank, tokens), F32),
            vmem((2 * rank, m), F32),
            vmem((rank, m), F32),
            vmem((2 * nx, eighth, m), F32),
            vmem((ny, eighth, m), F32),
            vmem((rank, m), F32),
            vmem((rank, m + 128), F32),
            vmem((count, rank, y_width), F32),
            vmem((count, half, y_width), F32),
            vmem((pairs, nx, ny, eighth, y_width), F32),
            vmem((pairs, ny, ny, eighth, y_width), F32),
            vmem((pairs, ny, half, y_width), F32),
            vmem((pairs, nx, half, y_width), F32),
            vmem((count, rank, y_width), F32),
            vmem((nz, 8, 128), F32),
            vmem((2, 8, 128), F32),
            vmem((nc, rank, w), F32),
            vmem((rank, bk), F32),
            vmem((rank, bk), F32),
            dma((4, nc)),
            dma((nc,)),
            dma((2, hop, nc)),
            dma((2, hop, nc)),
            dma((3, max(2 * nx, ny))),
            dma((3, max(2 * nx, ny))),
            dma((nc // 2, 4, max(nx, ny))),
            dma((nc // 2, 4, max(nx, ny))),
            dma((nc,)),
            dma((nc,)),
            dma((nz,)),
            dma((nz,)),
            dma((nx + ny + 1,)),
            dma((nx + ny + 1,)),
        ],
        compiler_params=pltpu.CompilerParams(
            collective_id=0, has_side_effects=True, vmem_limit_bytes=58 * 2**20
        ),
    )(heads_out, grad_out, error, q_warm)
    parts = 6 if m % 96 == 0 else 4
    return pl.pallas_call(
        hand_over,
        out_shape=outs,
        in_specs=[hbm] * 3,
        out_specs=(hbm,) * 3,
        scratch_shapes=[vmem(out.shape, out.dtype) for out in outs] + [dma((parts + 2,)), dma((parts + 2,))],
        compiler_params=pltpu.CompilerParams(vmem_limit_bytes=60 * 2**20),
    )(*results)


def solution(mesh, ny=4, nx=4):
    placed = (
        P("dp", "tensor"),
        P(("dp", "tensor"), None),
        P("dp", "tensor", None),
        P("tensor", None, None),
    )
    return jax.shard_map(
        functools.partial(shards, (ny, nx, mesh.shape["tensor"])),
        mesh=mesh,
        in_specs=placed,
        out_specs=(P(None, "tensor"), P("tensor", None, "dp"), P("dp", "tensor", None)),
        check_vma=False,
    )
```
